256 devices in a mesh: row: 16 (over z, core), col: 16 (over x, y).
Axes of the slice: x: 4, y: 4, z: 8, core: 2. Of those that a mesh axis runs over, the one named last changes fastest.
Arguments:
- source: bfloat16 [262144, 128], P('row'), may hold values from -36 to 36
- target: bfloat16 [131072, 128], P('col'), may hold values from -36 to 36
- log_source: float32 [262144], P('row'), may hold values from -2 to 2
- log_target: float32 [131072], P('col'), may hold values from -2 to 2
- support: int32 [1024, 16], P('row', 'col'), may hold values from 0 to 511, as said below
- counts: int32 [1024, 16], P('row', 'col'), may hold values from 0 to 1, as said below
Outputs:
- potential_row: float32 [262144], P('row')
- potential_col: float32 [131072], P('col')
The draws below stay inside these ranges and needn't reach their ends.
Inputs may be any that keep to these rules, and one draw needn't show every extreme that they name: `support`: slots 1 * d to 1 * d + 1 - 1 of a row block name column blocks d * 32 to (d + 1) * 32 - 1 of column device d; the live ones among them are distinct. Every column block is named by a live slot of some row block. `counts`: every row block has a live slot. In every draw each column device d has a row block whose slot d is live.
All inputs are finite; a program needn't handle non-finite values.
Results may differ from the reference program's by a relative error of at most 0.012.
Values sent between devices are 32-bit elements; how exact they have to be, the bound alone decides.
A program may use at most 64 MiB of HBM per device.

```python
import jax
import jax.numpy as jnp
from jax import lax

E = 128
BS = 256
KD = 1
ITERS = 2
RB_DEV = 64
CB_DEV = 32
NRB = 1024
NCB = 512
NS = 262144
NT = 131072
N_ROW = 16
N_COL = 16


def embed_rows(key, row_total, spread):
    key_normal, key_scale = jax.random.split(key)
    values = jnp.clip(jax.random.normal(key_normal, (row_total, E), jnp.float32), -6.0, 6.0)
    row_scale = jnp.exp(jax.random.uniform(key_scale, (row_total, 1), jnp.float32, 0.0, spread))
    return values * row_scale


def support_parts(key):
    keys = jax.random.split(key, 7)
    level = jax.random.randint(keys[0], (N_ROW, N_COL), 1, 4)
    level_rows = jnp.repeat(level, RB_DEV, axis=0)
    tries = jax.random.randint(keys[1], (NRB, N_COL, KD), 0, 4)
    live_count = jnp.sum((tries < level_rows[:, :, None]).astype(jnp.int32), axis=2)
    noise = jax.random.randint(keys[2], (NRB, N_COL), 0, 65536) * NRB + jnp.arange(NRB, dtype=jnp.int32)[:, None]
    order_rank = jnp.argsort(jnp.argsort(noise, axis=0), axis=0).astype(jnp.int32)
    covering = order_rank < CB_DEV
    live_count = jnp.where(covering, jnp.maximum(live_count, 1), live_count)
    anchor = jax.random.randint(keys[3], (NRB,), 0, N_COL)
    live_count = jnp.where(jnp.arange(N_COL, dtype=jnp.int32)[None, :] == anchor[:, None], jnp.maximum(live_count, 1), live_count)
    full_row = jax.random.randint(keys[4], (N_COL,), 0, NRB)
    live_count = jnp.where(jnp.arange(NRB, dtype=jnp.int32)[:, None] == full_row[None, :], KD, live_count)
    start_col = jax.random.randint(keys[5], (NRB, N_COL), 0, CB_DEV)
    start_col = jnp.where(covering, order_rank, start_col)
    gaps = 1 + jax.random.randint(keys[6], (NRB, N_COL, KD), 0, max(CB_DEV // KD, 1))
    offsets = jnp.cumsum(gaps, axis=2) - gaps
    within_dev = (start_col[:, :, None] + offsets) % CB_DEV
    columns = within_dev + jnp.arange(N_COL, dtype=jnp.int32)[None, :, None] * CB_DEV
    return (columns.reshape(NRB, N_COL * KD).astype(jnp.int32), live_count.astype(jnp.int32))


def draw_source(key, part):
    key = jax.random.fold_in(key, 11)
    spread = 0.0
    return embed_rows(key, NS, spread).astype(jnp.bfloat16)


def draw_target(key, part):
    key = jax.random.fold_in(key, 12)
    spread = 0.0
    return embed_rows(key, NT, spread).astype(jnp.bfloat16)


def draw_support(key, part):
    columns, live_count = support_parts(key)
    return columns


def draw_counts(key, part):
    columns, live_count = support_parts(key)
    return live_count


def block_levels(stream_key, shape, cuts, low, high):
    gain = 1.0
    for dim, blocks in cuts:
        heights = jax.random.uniform(jax.random.fold_in(jax.random.fold_in(stream_key, 6), dim), (blocks,), jnp.float32, low / len(cuts), high / len(cuts))
        gain = gain * jnp.repeat(jnp.exp(heights), shape[dim] // blocks).reshape((-1,) + (1,) * (len(shape) - 1 - dim))
    return gain


def setup_inputs(seed: int = 0) -> dict:
    arg_keys = jax.random.split(jax.random.key(seed), 7)
    return {
        "source": draw_source(jax.random.fold_in(arg_keys[6], 71), 0),
        "target": draw_target(jax.random.fold_in(arg_keys[6], 71), 0),
        "log_source": jnp.clip(jax.random.uniform(arg_keys[2], (NS,), jnp.float32, -2.0, 2.0) * block_levels(arg_keys[2], (NS,), ((0, 16),), -0.4, 0.0), -2.0, 2.0),
        "log_target": jnp.clip(jax.random.uniform(arg_keys[3], (NT,), jnp.float32, -2.0, 2.0) * block_levels(arg_keys[3], (NT,), ((0, 16),), -0.4, 0.0), -2.0, 2.0),
        "support": draw_support(jax.random.fold_in(arg_keys[6], 71), 0),
        "counts": draw_counts(jax.random.fold_in(arg_keys[6], 71), 0),
    }


entropic = 0.1
floor_value = -1.0e30


def slot_live(support, counts):
    slot_index = jnp.arange(support.shape[1], dtype=jnp.int32)
    device_of = slot_index // KD
    within = slot_index % KD
    return within[None, :] < counts[:, device_of]


def build_tiles(source, target, support):
    row_blocks = source.reshape(NRB, BS, E)
    col_blocks = target.reshape(NCB, BS, E)
    row_norms = jnp.sum(jnp.square(row_blocks.astype(jnp.float32)), axis=-1)
    col_norms = jnp.sum(jnp.square(col_blocks.astype(jnp.float32)), axis=-1)

    def one_row(pieces):
        row_block, norms_here, columns = pieces
        picked = col_blocks[columns].astype(jnp.float32)
        products = jnp.einsum("be,sce->sbc", row_block.astype(jnp.float32), picked)
        summed = norms_here[None, :, None] + col_norms[columns][:, None, :] - 2.0 * products
        return (summed / E).astype(jnp.bfloat16)

    return lax.map(one_row, (row_blocks, row_norms, support))


def row_potential(tiles, support, live_slots, log_source, potential_col):
    col_pot = potential_col.reshape(NCB, BS)

    def one_row(pieces):
        tile, columns, slot_ok, weights = pieces
        scores = (col_pot[columns][:, None, :] - tile.astype(jnp.float32)) / entropic
        scores = jnp.where(slot_ok[:, None, None], scores, floor_value)
        peak = jnp.max(scores, axis=(0, 2))
        summed = jnp.sum(jnp.where(slot_ok[:, None, None], jnp.exp(scores - peak[None, :, None]), 0.0), axis=(0, 2))
        return entropic * weights - entropic * (peak + jnp.log(summed))

    return lax.map(one_row, (tiles, support, live_slots, log_source.reshape(NRB, BS))).reshape(-1)


def col_potential(tiles, support, live_slots, log_target, potential_row):
    row_pot = potential_row.reshape(NRB, BS)
    slot_target = jnp.where(live_slots, support, NCB).astype(jnp.int32)
    initial = (jnp.full((NCB + 1, BS), floor_value, jnp.float32), jnp.zeros((NCB + 1, BS), jnp.float32))

    def one_row(running, pieces):
        tile, columns, slot_ok, values = pieces
        scores = (values[None, :, None] - tile.astype(jnp.float32)) / entropic
        peak = jnp.max(scores, axis=1)
        summed = jnp.sum(jnp.exp(scores - peak[:, None, :]), axis=1)
        peak = jnp.where(slot_ok[:, None], peak, floor_value)
        summed = jnp.where(slot_ok[:, None], summed, 0.0)
        prior_peak = running[0][columns]
        prior_sum = running[1][columns]
        new_peak = jnp.maximum(prior_peak, peak)
        new_sum = prior_sum * jnp.exp(prior_peak - new_peak) + summed * jnp.exp(peak - new_peak)
        return (running[0].at[columns].set(new_peak), running[1].at[columns].set(new_sum)), None

    (peak, summed), _ = lax.scan(one_row, initial, (tiles, slot_target, live_slots, row_pot))
    result = entropic * log_target.reshape(NCB, BS) - entropic * (peak[:NCB] + jnp.log(summed[:NCB]))
    return result.reshape(-1)


def reference(source, target, log_source, log_target, support, counts):
    live_slots = slot_live(support, counts)
    tiles = build_tiles(source, target, support)
    potential_col = jnp.zeros((NT,), jnp.float32)
    potential_row = jnp.zeros((NS,), jnp.float32)
    for iteration in range(ITERS):
        potential_row = row_potential(tiles, support, live_slots, log_source, potential_col)
        potential_col = col_potential(tiles, support, live_slots, log_target, potential_row)
    return potential_row, potential_col
```

```python
import functools
import math

import jax
import jax.numpy as jnp
from jax import lax
from jax.experimental import pallas as pl
from jax.experimental.pallas import tpu as pltpu
from jax.sharding import PartitionSpec as P

BS = 256
ITERS = 2
entropic = 0.1
floor_value = -1e30
LOG2E = math.log2(math.e)
SCALE = LOG2E / entropic
MESH = pl.DeviceIdType.MESH
GROUP = 4


def dot_nt(a, b):
    return lax.dot_general(a, b, (((1,), (1,)), ((), ())), preferred_element_type=jnp.float32)


def lane_column(row):
    return jnp.transpose(jnp.broadcast_to(row, (128, 128)))


def partial_lse(scores):
    stacked = scores.reshape(BS // 8, 8, 128)
    peak = jnp.max(stacked, axis=0)
    return peak + LOG2E * jnp.log(jnp.sum(jnp.exp2(stacked - peak[None]), axis=0))


def stacked_lse(parts):
    peak = functools.reduce(jnp.maximum, parts)
    total = functools.reduce(jnp.add, [jnp.exp2(part - peak) for part in parts])
    return peak + LOG2E * jnp.log(total)


def kernel(
    n_row, n_col,
    sup, cnt, src_hbm, tgt_hbm, ls, lt,
    f_out, g_out,
    src, tgt, dots_qp, dots_pq, gcol, fcol, part8, part16, key,
    lrow, rs_row, fall, lcol, lpart, rs_col, gall, rnorm, cnorm,
    tgt_sem, src_sem,
    rs_row_send, rs_row_recv, ag_row_send, ag_row_recv,
    rs_col_send, rs_col_recv, ag_col_send, ag_col_recv,
):
    row_count = src.shape[0]
    col_count = tgt.shape[0]
    embed = src.shape[2]
    my_row, my_col = lax.axis_index("row"), lax.axis_index("col")
    first_block = my_col * col_count
    dot_scale = 2.0 * SCALE / embed

    tgt_copy = pltpu.make_async_copy(tgt_hbm, tgt, tgt_sem)
    tgt_copy.start()

    def src_copy(c):
        here = pl.ds(c * GROUP, GROUP)
        return pltpu.make_async_copy(src_hbm.at[here], src.at[here], src_sem.at[c])

    for c in range(n_col):
        src_copy(c).start()

    barrier = pltpu.get_barrier_semaphore()
    for o in range(1, n_col):
        pl.semaphore_signal(barrier, inc=1, device_id=(my_row, lax.rem(my_col + o, n_col)), device_id_type=MESH)
    for o in range(1, n_row):
        pl.semaphore_signal(barrier, inc=1, device_id=(lax.rem(my_row + o, n_row), my_col), device_id_type=MESH)

    def block_of(i):
        return jnp.clip(sup[i, 0] - first_block, 0, col_count - 1)

    tgt_copy.wait()

    @pl.loop(0, n_row)
    def _(o):
        for a in range(2):
            block = tgt[2 * o + a].astype(jnp.float32)
            square = block * block
            high = square.astype(jnp.bfloat16)
            low = (square - high.astype(jnp.float32)).astype(jnp.bfloat16)
            ones = jnp.ones((8, embed), jnp.bfloat16)
            across = (dot_nt(ones, high) + dot_nt(ones, low)) * (1.0 / embed)
            for h in range(2):
                cnorm[o, pl.ds(2 * a + h, 1), :] = across[0:1, h * 128:(h + 1) * 128]
            down = jnp.sum(square, axis=1, keepdims=True) * (-SCALE / embed)
            gcol[2 * o + a] = jnp.broadcast_to(down, (BS, 128))

    pl.semaphore_wait(barrier, n_row + n_col - 2)

    def rs_row_copy(it, c):
        return pltpu.make_async_remote_copy(
            src_ref=lrow.at[it, c], dst_ref=rs_row.at[it, my_col],
            send_sem=rs_row_send.at[it, c], recv_sem=rs_row_recv.at[it, my_col],
            device_id=(my_row, c), device_id_type=MESH)

    def ag_row_copy(it, peer):
        return pltpu.make_async_remote_copy(
            src_ref=fall.at[it, my_col], dst_ref=fall.at[it, my_col],
            send_sem=ag_row_send.at[it, peer], recv_sem=ag_row_recv.at[it, my_col],
            device_id=(my_row, peer), device_id_type=MESH)

    def rs_col_copy(it, r):
        return pltpu.make_async_remote_copy(
            src_ref=lcol.at[it, r], dst_ref=rs_col.at[it, my_row],
            send_sem=rs_col_send.at[it, r], recv_sem=rs_col_recv.at[it, my_row],
            device_id=(r, my_col), device_id_type=MESH)

    def ag_col_copy(it, peer):
        return pltpu.make_async_remote_copy(
            src_ref=gall.at[it, my_row], dst_ref=gall.at[it, my_row],
            send_sem=ag_col_send.at[it, peer], recv_sem=ag_col_recv.at[it, my_row],
            device_id=(peer, my_col), device_id_type=MESH)

    def arrived(buffer, sem, it, slot):
        pltpu.make_async_copy(buffer.at[it, slot], buffer.at[it, slot], sem.at[it, slot]).wait()

    def row_chunk(it, c):
        for t in range(GROUP):
            i = GROUP * c + t
            block = block_of(i)
            dead = jnp.where(cnt[i, 0] > 0, 0.0, floor_value)
            if it == 0:
                dots_qp[i] = dot_nt(tgt[block], src[i]) * dot_scale
            for h in range(2):
                scores = dots_qp[i, :, h * 128:(h + 1) * 128] + gcol[block]
                part8[pl.ds(8 * (2 * t + h), 8), :] = partial_lse(scores) + dead
        lrow[it, c] = stacked_lse([part8[pl.ds(s, 8, stride=8), :] for s in range(8)])

        @pl.when(c != my_col)
        def _():
            rs_row_copy(it, c).start()

        @pl.when(c == my_col)
        def _():
            rs_row[it, my_col] = lrow[it, c]

    def row_owner(it):
        for o in range(1, n_col):
            arrived(rs_row, rs_row_recv, it, lax.rem(my_col + o, n_col))
        total = stacked_lse([rs_row[it, d] for d in range(n_col)])
        fall[it, my_col] = ls[my_col] * LOG2E - total
        for o in range(1, n_col):
            ag_row_copy(it, lax.rem(my_col + o, n_col)).start()

    def col_chunk(it, c):
        @pl.when(c != my_col)
        def _():
            arrived(fall, ag_row_recv, it, c)

        for t in range(GROUP):
            i = GROUP * c + t
            for h in range(2):
                fcol[h * 128:(h + 1) * 128, :] = lane_column(fall[it, c, pl.ds(2 * t + h, 1), :])
            for h in range(2):
                scores = dots_pq[i, :, h * 128:(h + 1) * 128] + fcol[...]
                part8[pl.ds(8 * (GROUP * h + t), 8), :] = partial_lse(scores)
        lpart[c] = stacked_lse([part8[pl.ds(s, 8, stride=8), :] for s in range(8)])

    def col_send(it, r):
        for a in range(2):
            mine = jnp.where(key[...] == 2 * r + a, lpart[...], floor_value)
            peak = jnp.max(mine, axis=0)
            total = jnp.sum(jnp.exp2(mine - peak[None]), axis=0)
            part16[pl.ds(8 * a, 8), :] = peak + LOG2E * jnp.log(total)
        lcol[it, r] = stacked_lse([part16[pl.ds(s, 4, stride=4), :] for s in range(4)])

        @pl.when(r != my_row)
        def _():
            rs_col_copy(it, r).start()

        @pl.when(r == my_row)
        def _():
            rs_col[it, my_row] = lcol[it, r]

    def col_owner(it):
        for o in range(1, n_row):
            arrived(rs_col, rs_col_recv, it, lax.rem(my_row + o, n_row))
        total = stacked_lse([rs_col[it, d] for d in range(n_row)])
        gall[it, my_row] = lt[my_row] * LOG2E - total
        for o in range(1, n_row):
            ag_col_copy(it, lax.rem(my_row + o, n_row)).start()

    def make_chunk(c):
        sublane = lax.broadcasted_iota(jnp.int32, (8, 128), 0)
        names = jnp.full((8, 128), -1, jnp.int32)
        for t in range(GROUP):
            i = GROUP * c + t
            block = block_of(i)
            dots_pq[i] = dot_nt(src[i], tgt[block]) * dot_scale
            name = jnp.where(cnt[i, 0] > 0, block, -1)
            names = jnp.where(lax.rem(sublane, GROUP) == t, name, names)
            piece = src[i].astype(jnp.float32)
            square = piece * piece
            high = square.astype(jnp.bfloat16)
            low = (square - high.astype(jnp.float32)).astype(jnp.bfloat16)
            ones = jnp.ones((8, embed), jnp.bfloat16)
            across = (dot_nt(ones, high) + dot_nt(ones, low)) * (1.0 / embed)
            for h in range(2):
                rnorm[c, pl.ds(2 * t + h, 1), :] = across[0:1, h * 128:(h + 1) * 128]
        key[c] = names

    for it in range(ITERS):
        @pl.loop(0, n_col)
        def _(c):
            if it == 0:
                src_copy(c).wait()
            row_chunk(it, c)

        if it == 0:
            pl.loop(0, n_col)(make_chunk)
        row_owner(it)

        @pl.loop(0, n_col)
        def _(c):
            col_chunk(it, c)

        @pl.loop(0, n_row)
        def _(r):
            col_send(it, r)

        for o in range(1, n_col):
            peer = lax.rem(my_col + o, n_col)
            rs_row_copy(it, peer).wait_send()
            ag_row_copy(it, peer).wait_send()
        col_owner(it)
        if it == ITERS - 1:
            f_out[...] = fall[it] * (1.0 / SCALE) + rnorm[...]

        @pl.loop(0, n_row)
        def _(r):
            @pl.when(r != my_row)
            def _():
                arrived(gall, ag_col_recv, it, r)

            if it < ITERS - 1:
                for a in range(2):
                    for h in range(2):
                        gcol[2 * r + a, h * 128:(h + 1) * 128, :] = lane_column(gall[it, r, pl.ds(2 * a + h, 1), :])

        for o in range(1, n_row):
            peer = lax.rem(my_row + o, n_row)
            rs_col_copy(it, peer).wait_send()
            ag_col_copy(it, peer).wait_send()
    g_out[...] = gall[ITERS - 1] * (1.0 / SCALE) + cnorm[...]


def on_device(n_row, n_col, source, target, log_source, log_target, support, counts):
    row_count = support.shape[0]
    embed = source.shape[1]
    col_count = target.shape[0] // BS
    f32 = jnp.float32
    smem = pl.BlockSpec(memory_space=pltpu.SMEM)
    vmem = pl.BlockSpec(memory_space=pltpu.VMEM)
    hbm = pl.BlockSpec(memory_space=pl.ANY)
    dma = pltpu.SemaphoreType.DMA
    row_shape, col_shape = (n_col, 8, 128), (n_row, 4, 128)
    f, g = pl.pallas_call(
        functools.partial(kernel, n_row, n_col),
        out_shape=(jax.ShapeDtypeStruct(row_shape, f32), jax.ShapeDtypeStruct(col_shape, f32)),
        in_specs=[smem, smem, hbm, hbm, vmem, vmem],
        out_specs=(vmem, vmem),
        scratch_shapes=[
            pltpu.VMEM((row_count, BS, embed), jnp.bfloat16),
            pltpu.VMEM((col_count, BS, embed), jnp.bfloat16),
            pltpu.VMEM((row_count, BS, BS), f32),
            pltpu.VMEM((row_count, BS, BS), f32),
            pltpu.VMEM((col_count, BS, 128), f32),
            pltpu.VMEM((BS, 128), f32),
            pltpu.VMEM((64, 128), f32),
            pltpu.VMEM((16, 128), f32),
            pltpu.VMEM(row_shape, jnp.int32),
            pltpu.VMEM((ITERS,) + row_shape, f32),
            pltpu.VMEM((ITERS,) + row_shape, f32),
            pltpu.VMEM((ITERS,) + row_shape, f32),
            pltpu.VMEM((ITERS,) + col_shape, f32),
            pltpu.VMEM(row_shape, f32),
            pltpu.VMEM((ITERS,) + col_shape, f32),
            pltpu.VMEM((ITERS,) + col_shape, f32),
            pltpu.VMEM(row_shape, f32),
            pltpu.VMEM(col_shape, f32),
            dma(()),
            dma((n_col,)),
        ] + [dma((ITERS, n_col))] * 4 + [dma((ITERS, n_row))] * 4,
        compiler_params=pltpu.CompilerParams(
            collective_id=0, has_side_effects=True, vmem_limit_bytes=56 * 1024 * 1024),
    )(
        support, counts,
        source.reshape(row_count, BS, embed), target.reshape(col_count, BS, embed),
        log_source.reshape(row_shape), log_target.reshape(col_shape),
    )
    return f.reshape(-1), g.reshape(-1)


def solution(mesh):
    placed = (P("row", None), P("col", None), P("row"), P("col"), P("row", "col"), P("row", "col"))
    body = functools.partial(on_device, mesh.shape["row"], mesh.shape["col"])
    return jax.shard_map(
        body, mesh=mesh, in_specs=placed, out_specs=(P("row"), P("col")), check_vma=False
    )
```

```python
import functools
import math

import jax
import jax.numpy as jnp
from jax import lax
from jax.experimental import pallas as pl
from jax.experimental.pallas import tpu as pltpu
from jax.sharding import PartitionSpec as P

BS = 256
ITERS = 2
entropic = 0.1
floor_value = -1e30
LOG2E = math.log2(math.e)
SCALE = LOG2E / entropic
MESH = pl.DeviceIdType.MESH
TILES = 4
GROUPS = 4
PART = 64


def dot_nt(a, b):
    return lax.dot_general(a, b, (((1,), (1,)), ((), ())), preferred_element_type=jnp.float32)


def lane_column(row):
    return jnp.transpose(jnp.broadcast_to(row, (128, 128)))


def tree(op, parts):
    parts = list(parts)
    while len(parts) > 1:
        paired = [op(a, b) for a, b in zip(parts[::2], parts[1::2])]
        parts = paired + parts[len(parts) - len(parts) % 2:]
    return parts[0]


def merged(pairs):
    peak = tree(jnp.maximum, [p for p, _ in pairs])
    return peak, tree(jnp.add, [s * jnp.exp2(p - peak) for p, s in pairs])


def log_sum(pair):
    return pair[0] + LOG2E * jnp.log(pair[1])


def merged_logs(parts):
    peak = tree(jnp.maximum, parts)
    return peak + LOG2E * jnp.log(tree(jnp.add, [jnp.exp2(part - peak) for part in parts]))


def tile_pairs(products, offsets):
    pairs = []
    for k in range(0, BS, PART):
        scores = (products(k) + offsets(k)).reshape(PART // 8, 8, 128)
        peak = jnp.max(scores, axis=0)
        pairs.append((peak, jnp.sum(jnp.exp2(scores - peak[None]), axis=0)))
    return merged(pairs)


def sublane_pairs(peaks, sums, count, stride):
    return merged([
        (peaks[pl.ds(s, count, stride=stride), :], sums[pl.ds(s, count, stride=stride), :])
        for s in range(stride)])


def squares(block):
    wide = block.astype(jnp.float32)
    return wide * wide


def norms_across(block):
    square = squares(block)
    high = square.astype(jnp.bfloat16)
    low = (square - high.astype(jnp.float32)).astype(jnp.bfloat16)
    ones = jnp.ones((8, block.shape[1]), jnp.bfloat16)
    return ((dot_nt(ones, high) + dot_nt(ones, low)) * (1.0 / block.shape[1]))[0:1]


def block_of(r, i):
    return jnp.clip(r.sup[0, i] - r.first_block, 0, r.tgt.shape[0] - 1)


def start_columns(r, o):
    for a in range(4):
        block = r.tgt[4 * o + a]
        down = jnp.sum(squares(block), axis=1, keepdims=True) * (-SCALE / block.shape[1])
        r.gcol[4 * o + a] = jnp.broadcast_to(down, (BS, 128))


def row_group(r, it, g, chunks, place):
    for k in range(chunks):
        c = chunks * g + k
        for t in range(TILES):
            i = TILES * c + t
            block = block_of(r, i)
            dead = jnp.where(r.cnt[0, i] > 0, 0.0, floor_value)
            if it == 0:
                made = dot_nt(r.tgt[block], r.src[i]) * (2.0 * SCALE / r.src.shape[2])
                r.dots_qp[i] = made
            for h in range(2):
                lanes = slice(h * 128, (h + 1) * 128)
                if it == 0:
                    products = lambda k: made[k:k + PART, lanes]
                else:
                    products = lambda k: r.dots_qp[i, k:k + PART, lanes]
                peak, total = tile_pairs(products, lambda k: r.gcol[block, k:k + PART, :])
                here = pl.ds(64 * k + 8 * (2 * t + h), 8)
                r.peaks[here, :] = peak + dead
                r.sums[here, :] = total
        at = pl.ds(64 * k, 64)
        place(c, log_sum(sublane_pairs(r.peaks.at[at], r.sums.at[at], 8, 8)))


def make_group(r, g, chunks):
    sublane = lax.broadcasted_iota(jnp.int32, (8, 128), 0)
    for k in range(chunks):
        c = chunks * g + k
        names = jnp.full((8, 128), -1, jnp.int32)
        for t in range(TILES):
            i = TILES * c + t
            block = block_of(r, i)
            r.dots_pq[i] = dot_nt(r.src[i], r.tgt[block]) * (2.0 * SCALE / r.src.shape[2])
            name = jnp.where(r.cnt[0, i] > 0, block, -1)
            names = jnp.where(lax.rem(sublane, TILES) == t, name, names)
        r.key[c] = names


def col_group(r, g, chunks):
    for k in range(chunks):
        c = chunks * g + k
        for t in range(TILES):
            i = TILES * c + t
            down = [lane_column(r.fall[c, pl.ds(2 * t + h, 1), :]) for h in range(2)]
            for h in range(2):
                peak, total = tile_pairs(
                    lambda k: r.dots_pq[i, k:k + PART, h * 128:(h + 1) * 128],
                    lambda k: down[k // 128][k % 128:k % 128 + PART])
                here = pl.ds(64 * k + 8 * (TILES * h + t), 8)
                r.peaks[here, :] = peak
                r.sums[here, :] = total
        at = pl.ds(64 * k, 64)
        r.lpart[c] = log_sum(sublane_pairs(r.peaks.at[at], r.sums.at[at], 8, 8))


def merge_columns(r, chunk):
    for u in range(4):
        mine = jnp.where(r.key[...] == 4 * chunk + u, r.lpart[...], floor_value)
        peak = jnp.max(mine, axis=0)
        here = pl.ds(8 * u, 8)
        r.peaks[here, :] = peak
        r.sums[here, :] = jnp.sum(jnp.exp2(mine - peak[None]), axis=0)
    return log_sum(sublane_pairs(r.peaks, r.sums, 8, 4))


def spread_columns(r, chunk, rows):
    for j in range(8):
        r.gcol[4 * chunk + j // 2, (j % 2) * 128:(j % 2 + 1) * 128, :] = lane_column(rows[j:j + 1])


REFS = (
    "sup", "cnt", "src_hbm", "tgt_hbm", "ls", "lt", "f_out", "g_out", "src", "tgt", "dots_qp", "dots_pq",
    "gcol", "peaks", "sums", "key", "fall", "lpart", "rnorm", "cnorm", "first", "second", "stage", "pair",
    "ring", "gall", "tgt_sem", "src_sem", "first_send", "first_recv", "second_send", "second_recv",
    "pair_send", "pair_recv", "ring_send", "ring_recv", "back_send", "back_recv",
)


class Refs:
    pass


def kernel(n_row, n_col, *refs):
    r = Refs()
    for name, ref in zip(REFS, refs, strict=True):
        setattr(r, name, ref)
    side = math.isqrt(n_col)
    depth = n_row // 2
    my_row, my_col = lax.axis_index("row"), lax.axis_index("col")
    my_x, my_y = my_col // side, lax.rem(my_col, side)
    my_z, my_core = my_row // 2, lax.rem(my_row, 2)
    other = 1 - my_core
    r.first_block = my_col * r.tgt.shape[0]
    chunks = n_col // GROUPS
    half = r.gall.shape[2]

    tgt_copy = pltpu.make_async_copy(r.tgt_hbm, r.tgt, r.tgt_sem)
    tgt_copy.start()

    def src_copy(g):
        here = pl.ds(g * chunks * TILES, chunks * TILES)
        return pltpu.make_async_copy(r.src_hbm.at[here], r.src.at[here], r.src_sem.at[g])

    for g in range(GROUPS):
        src_copy(g).start()

    def on_x(o):
        return (my_row, lax.rem(my_x + o, side) * side + my_y)

    def on_y(o):
        return (my_row, my_x * side + lax.rem(my_y + o, side))

    def on_z(o):
        return (lax.rem(my_z + o, depth) * 2 + my_core, my_col)

    sibling = (my_z * 2 + other, my_col)
    barrier = pltpu.get_barrier_semaphore()
    for o in range(1, depth):
        pl.semaphore_signal(barrier, inc=1, device_id=on_z(o), device_id_type=MESH)
    for o in range(1, side):
        pl.semaphore_signal(barrier, inc=1, device_id=on_x(o), device_id_type=MESH)
        pl.semaphore_signal(barrier, inc=1, device_id=on_y(o), device_id_type=MESH)
    pl.semaphore_signal(barrier, inc=1, device_id=sibling, device_id_type=MESH)

    def place_of(g, which):
        x_now = lax.rem(g + which, 2) == 0
        return x_now, jnp.where(x_now, my_x, my_y)

    def row_copy(it, g, which, o):
        buffer, send, recv = (r.first, r.first_send, r.first_recv) if which == 0 else (
            r.second, r.second_send, r.second_recv)
        x_now, me = place_of(g, which)
        (row, x_col), (_, y_col) = on_x(o), on_y(o)
        here = buffer.at[it, me, pl.ds(g * chunks, chunks)]
        return pltpu.make_async_remote_copy(
            src_ref=here, dst_ref=here, send_sem=send.at[it, g, o], recv_sem=recv.at[it, g, me],
            device_id=(row, jnp.where(x_now, x_col, y_col)), device_id_type=MESH)

    def row_arrived(it, g, which):
        buffer, recv = (r.first, r.first_recv) if which == 0 else (r.second, r.second_recv)
        _, me = place_of(g, which)
        for o in range(1, side):
            slot = lax.rem(me + o, side)
            here = buffer.at[it, slot, pl.ds(g * chunks, chunks)]
            pltpu.make_async_copy(here, here, recv.at[it, g, slot]).wait()

    def row_merged(it, g, which):
        buffer = r.first if which == 0 else r.second
        return merged_logs([buffer[it, d, pl.ds(g * chunks, chunks)] for d in range(side)])

    def pair_copy(it):
        return pltpu.make_async_remote_copy(
            src_ref=r.stage.at[it], dst_ref=r.pair.at[it, my_core],
            send_sem=r.pair_send.at[it], recv_sem=r.pair_recv.at[it],
            device_id=sibling, device_id_type=MESH)

    def ring_copy(it, o):
        here = r.ring.at[it, my_z]
        return pltpu.make_async_remote_copy(
            src_ref=here, dst_ref=here, send_sem=r.ring_send.at[it, o], recv_sem=r.ring_recv.at[it, my_z],
            device_id=on_z(o), device_id_type=MESH)

    def back_copy(it):
        here = r.gall.at[it, my_core]
        return pltpu.make_async_remote_copy(
            src_ref=here, dst_ref=here, send_sem=r.back_send.at[it], recv_sem=r.back_recv.at[it],
            device_id=sibling, device_id_type=MESH)

    tgt_copy.wait()
    pl.loop(0, r.tgt.shape[0] // 4)(lambda o: start_columns(r, o))

    for it in range(ITERS):
        @pl.loop(0, GROUPS)
        def _(g):
            if it == 0:
                src_copy(g).wait()
            _, me = place_of(g, 0)

            def place(c, value):
                r.first[it, me, c] = value

            row_group(r, it, g, chunks, place)
            if it == 0:
                @pl.when(g == 0)
                def _():
                    pl.semaphore_wait(barrier, 2 * (side - 1) + depth)

            for o in range(1, side):
                row_copy(it, g, 0, o).start()

        if it == 0:
            pl.loop(0, GROUPS // 2)(lambda g: make_group(r, g, chunks))

        @pl.loop(0, GROUPS)
        def _(g):
            row_arrived(it, g, 0)
            _, me = place_of(g, 1)
            r.second[it, me, pl.ds(g * chunks, chunks)] = row_merged(it, g, 0)
            for o in range(1, side):
                row_copy(it, g, 1, o).start()

        if it == 0:
            pl.loop(GROUPS // 2, GROUPS)(lambda g: make_group(r, g, chunks))

        @pl.loop(0, GROUPS)
        def _(g):
            row_arrived(it, g, 1)
            here = pl.ds(g * chunks, chunks)
            r.fall[here] = r.ls[here] * LOG2E - row_merged(it, g, 1)
            col_group(r, g, chunks)

        @pl.loop(0, half)
        def _(j):
            r.stage[it, j] = merge_columns(r, other * half + j)

        pair_copy(it).start()

        @pl.loop(0, half)
        def _(j):
            r.pair[it, my_core, j] = merge_columns(r, my_core * half + j)

        pair_copy(it).wait_recv()
        r.ring[it, my_z] = merged_logs([r.pair[it, 0], r.pair[it, 1]])
        far_first = sorted(range(1, depth), key=lambda o: -min(o, depth - o))
        for o in far_first:
            ring_copy(it, o).start()

        if it == 0:
            @pl.loop(0, n_col)
            def _(c):
                for t in range(TILES):
                    across = norms_across(r.src[TILES * c + t])
                    for h in range(2):
                        r.rnorm[c, pl.ds(2 * t + h, 1), :] = across[:, h * 128:(h + 1) * 128]

            @pl.loop(0, 2 * half)
            def _(c):
                for t in range(TILES):
                    across = norms_across(r.tgt[TILES * c + t])
                    for h in range(2):
                        r.cnorm[c, pl.ds(2 * t + h, 1), :] = across[:, h * 128:(h + 1) * 128]

        if it == ITERS - 1:
            r.f_out[...] = r.fall[...] * (1.0 / SCALE) + r.rnorm[...]

        @pl.loop(0, GROUPS)
        def _(g):
            for o in range(1, side):
                row_copy(it, g, 0, o).wait_send()
                row_copy(it, g, 1, o).wait_send()

        pair_copy(it).wait_send()

        for o in far_first:
            slot = lax.rem(my_z + o, depth)
            here = r.ring.at[it, slot]
            pltpu.make_async_copy(here, here, r.ring_recv.at[it, slot]).wait()
        r.gall[it, my_core] = (
            r.lt[pl.ds(my_core * half, half)] * LOG2E - merged_logs([r.ring[it, d] for d in range(depth)]))
        back_copy(it).start()

        def finish(core):
            if it < ITERS - 1:
                pl.loop(0, half)(lambda j: spread_columns(r, core * half + j, r.gall[it, core, j]))
            else:
                here = pl.ds(core * half, half)
                r.g_out[here] = r.gall[it, core] * (1.0 / SCALE) + r.cnorm[here]

        finish(my_core)
        for o in far_first:
            ring_copy(it, o).wait_send()
        back_copy(it).wait()
        finish(other)


def on_device(n_row, n_col, source, target, log_source, log_target, support, counts):
    row_count = support.shape[0]
    embed = source.shape[1]
    col_count = target.shape[0] // BS
    side = math.isqrt(n_col)
    depth = n_row // 2
    f32 = jnp.float32
    smem = pl.BlockSpec(memory_space=pltpu.SMEM)
    vmem = pl.BlockSpec(memory_space=pltpu.VMEM)
    hbm = pl.BlockSpec(memory_space=pl.ANY)
    dma = pltpu.SemaphoreType.DMA
    row_shape, col_shape = (row_count // TILES, 8, 128), (col_count // TILES, 8, 128)
    half_shape = (col_count // TILES // 2, 8, 128)
    gathered = TILES * 16 * row_count // (TILES * GROUPS)
    f, g = pl.pallas_call(
        functools.partial(kernel, n_row, n_col),
        out_shape=(jax.ShapeDtypeStruct(row_shape, f32), jax.ShapeDtypeStruct(col_shape, f32)),
        in_specs=[smem, smem, hbm, hbm, vmem, vmem],
        out_specs=(vmem, vmem),
        scratch_shapes=[
            pltpu.VMEM((row_count, BS, embed), jnp.bfloat16),
            pltpu.VMEM((col_count, BS, embed), jnp.bfloat16),
            pltpu.VMEM((row_count, BS, BS), f32),
            pltpu.VMEM((row_count, BS, BS), f32),
            pltpu.VMEM((col_count, BS, 128), f32),
            pltpu.VMEM((gathered, 128), f32),
            pltpu.VMEM((gathered, 128), f32),
            pltpu.VMEM(row_shape, jnp.int32),
            pltpu.VMEM(row_shape, f32),
            pltpu.VMEM(row_shape, f32),
            pltpu.VMEM(row_shape, f32),
            pltpu.VMEM(col_shape, f32),
            pltpu.VMEM((ITERS, side) + row_shape, f32),
            pltpu.VMEM((ITERS, side) + row_shape, f32),
            pltpu.VMEM((ITERS,) + half_shape, f32),
            pltpu.VMEM((ITERS, 2) + half_shape, f32),
            pltpu.VMEM((ITERS, depth) + half_shape, f32),
            pltpu.VMEM((ITERS, 2) + half_shape, f32),
            dma(()),
            dma((GROUPS,)),
            dma((ITERS, GROUPS, side)), dma((ITERS, GROUPS, side)),
            dma((ITERS, GROUPS, side)), dma((ITERS, GROUPS, side)),
            dma((ITERS,)), dma((ITERS,)),
            dma((ITERS, depth)), dma((ITERS, depth)),
            dma((ITERS,)), dma((ITERS,)),
        ],
        compiler_params=pltpu.CompilerParams(
            collective_id=0, has_side_effects=True, vmem_limit_bytes=56 * 1024 * 1024),
    )(
        support.T, counts.T,
        source.reshape(row_count, BS, embed), target.reshape(col_count, BS, embed),
        log_source.reshape(row_shape), log_target.reshape(col_shape),
    )
    return f.reshape(-1), g.reshape(-1)


def solution(mesh):
    placed = (P("row", None), P("col", None), P("row"), P("col"), P("row", "col"), P("row", "col"))
    body = functools.partial(on_device, mesh.shape["row"], mesh.shape["col"])
    return jax.shard_map(
        body, mesh=mesh, in_specs=placed, out_specs=(P("row"), P("col")), check_vma=False
    )
```

```python
import functools
import math

import jax
import jax.numpy as jnp
from jax import lax
from jax.experimental import pallas as pl
from jax.experimental.pallas import tpu as pltpu
from jax.sharding import PartitionSpec as P

BS = 256
ITERS = 2
entropic = 0.1
floor_value = -1e30
LOG2E = math.log2(math.e)
SCALE = LOG2E / entropic
MESH = pl.DeviceIdType.MESH
TILES = 4
GROUPS = 4
TGT_PARTS = 2
PART = 64


def dot_nt(a, b):
    return lax.dot_general(a, b, (((1,), (1,)), ((), ())), preferred_element_type=jnp.float32)


def lane_column(row):
    return jnp.transpose(jnp.broadcast_to(row, (128, 128)))


def tree(op, parts):
    parts = list(parts)
    while len(parts) > 1:
        paired = [op(a, b) for a, b in zip(parts[::2], parts[1::2])]
        parts = paired + parts[len(parts) - len(parts) % 2:]
    return parts[0]


def merged(pairs):
    peak = tree(jnp.maximum, [p for p, _ in pairs])
    return peak, tree(jnp.add, [s * jnp.exp2(p - peak) for p, s in pairs])


def log_sum(pair):
    return pair[0] + LOG2E * jnp.log(pair[1])


def merged_logs(parts):
    peak = tree(jnp.maximum, parts)
    return peak + LOG2E * jnp.log(tree(jnp.add, [jnp.exp2(part - peak) for part in parts]))


def tile_pairs(products, offsets):
    pairs = []
    for k in range(0, BS, PART):
        scores = (products(k) + offsets(k)).reshape(PART // 8, 8, 128)
        peak = jnp.max(scores, axis=0)
        pairs.append((peak, jnp.sum(jnp.exp2(scores - peak[None]), axis=0)))
    return merged(pairs)


def sublane_pairs(peaks, sums, count, stride):
    return merged([
        (peaks[pl.ds(s, count, stride=stride), :], sums[pl.ds(s, count, stride=stride), :])
        for s in range(stride)])


def squares(block):
    wide = block.astype(jnp.float32)
    return wide * wide


def norms_across(block):
    square = squares(block)
    high = square.astype(jnp.bfloat16)
    low = (square - high.astype(jnp.float32)).astype(jnp.bfloat16)
    ones = jnp.ones((8, block.shape[1]), jnp.bfloat16)
    return ((dot_nt(ones, high) + dot_nt(ones, low)) * (1.0 / block.shape[1]))[0:1]


def block_of(r, i):
    return jnp.clip(r.sup[0, i] - r.first_block, 0, r.tgt.shape[0] - 1)


def start_columns(r, o, count):
    for a in range(count):
        block = r.tgt[count * o + a]
        down = jnp.sum(squares(block), axis=1, keepdims=True) * (-SCALE / block.shape[1])
        r.gcol[count * o + a] = jnp.broadcast_to(down, (BS, 128))


def row_group(r, it, g, chunks, place):
    for k in range(chunks):
        c = chunks * g + k
        for t in range(TILES):
            i = TILES * c + t
            block = block_of(r, i)
            dead = jnp.where(r.cnt[0, i] > 0, 0.0, floor_value)
            if it == 0:
                made = dot_nt(r.tgt[block], r.src[i]) * (2.0 * SCALE / r.src.shape[2])
                r.dots_qp[i] = made
            for h in range(2):
                lanes = slice(h * 128, (h + 1) * 128)
                if it == 0:
                    products = lambda k: made[k:k + PART, lanes]
                else:
                    products = lambda k: r.dots_qp[i, k:k + PART, lanes]
                peak, total = tile_pairs(products, lambda k: r.gcol[block, k:k + PART, :])
                here = pl.ds(64 * k + 8 * (2 * t + h), 8)
                r.peaks[here, :] = peak + dead
                r.sums[here, :] = total
        at = pl.ds(64 * k, 64)
        place(c, log_sum(sublane_pairs(r.peaks.at[at], r.sums.at[at], 8, 8)))


def make_group(r, g, chunks):
    sublane = lax.broadcasted_iota(jnp.int32, (8, 128), 0)
    for k in range(chunks):
        c = chunks * g + k
        names = jnp.full((8, 128), -1, jnp.int32)
        for t in range(TILES):
            i = TILES * c + t
            block = block_of(r, i)
            r.dots_pq[i] = dot_nt(r.src[i], r.tgt[block]) * (2.0 * SCALE / r.src.shape[2])
            name = jnp.where(r.cnt[0, i] > 0, block, -1)
            names = jnp.where(lax.rem(sublane, TILES) == t, name, names)
        r.key[c] = names


def col_group(r, g, chunks):
    for k in range(chunks):
        c = chunks * g + k
        for t in range(TILES):
            i = TILES * c + t
            down = [lane_column(r.fall[c, pl.ds(2 * t + h, 1), :]) for h in range(2)]
            for h in range(2):
                peak, total = tile_pairs(
                    lambda k: r.dots_pq[i, k:k + PART, h * 128:(h + 1) * 128],
                    lambda k: down[k // 128][k % 128:k % 128 + PART])
                here = pl.ds(64 * k + 8 * (TILES * h + t), 8)
                r.peaks[here, :] = peak
                r.sums[here, :] = total
        at = pl.ds(64 * k, 64)
        r.lpart[c] = log_sum(sublane_pairs(r.peaks.at[at], r.sums.at[at], 8, 8))


def merge_columns(r, chunk):
    for u in range(4):
        mine = jnp.where(r.key[...] == 4 * chunk + u, r.lpart[...], floor_value)
        peak = jnp.max(mine, axis=0)
        here = pl.ds(8 * u, 8)
        r.peaks[here, :] = peak
        r.sums[here, :] = jnp.sum(jnp.exp2(mine - peak[None]), axis=0)
    return log_sum(sublane_pairs(r.peaks, r.sums, 8, 4))


def spread_columns(r, chunk, rows):
    for j in range(8):
        r.gcol[4 * chunk + j // 2, (j % 2) * 128:(j % 2 + 1) * 128, :] = lane_column(rows[j:j + 1])


REFS = (
    "sup", "cnt", "src_hbm", "tgt_hbm", "ls", "lt", "f_out", "g_out", "src", "tgt", "dots_qp", "dots_pq",
    "gcol", "peaks", "sums", "key", "fall", "lpart", "rnorm", "cnorm", "first", "second", "stage", "pair",
    "ring", "gall", "tgt_sem", "src_sem", "first_send", "first_recv", "second_send", "second_recv",
    "pair_send", "pair_recv", "ring_send", "ring_recv", "back_send", "back_recv",
)


class Refs:
    pass


def kernel(n_row, n_col, *refs):
    r = Refs()
    for name, ref in zip(REFS, refs, strict=True):
        setattr(r, name, ref)
    side = math.isqrt(n_col)
    depth = n_row // 2
    my_row, my_col = lax.axis_index("row"), lax.axis_index("col")
    my_x, my_y = my_col // side, lax.rem(my_col, side)
    my_z, my_core = my_row // 2, lax.rem(my_row, 2)
    other = 1 - my_core
    r.first_block = my_col * r.tgt.shape[0]
    chunks = n_col // GROUPS
    half = r.gall.shape[2]

    tgt_part = r.tgt.shape[0] // TGT_PARTS

    def tgt_copy(o):
        here = pl.ds(o * tgt_part, tgt_part)
        return pltpu.make_async_copy(r.tgt_hbm.at[here], r.tgt.at[here], r.tgt_sem.at[o])

    for o in range(TGT_PARTS):
        tgt_copy(o).start()

    def src_copy(g):
        here = pl.ds(g * chunks * TILES, chunks * TILES)
        return pltpu.make_async_copy(r.src_hbm.at[here], r.src.at[here], r.src_sem.at[g])

    for g in range(GROUPS):
        src_copy(g).start()

    def on_x(o):
        return (my_row, lax.rem(my_x + o, side) * side + my_y)

    def on_y(o):
        return (my_row, my_x * side + lax.rem(my_y + o, side))

    def on_z(o):
        return (lax.rem(my_z + o, depth) * 2 + my_core, my_col)

    sibling = (my_z * 2 + other, my_col)
    barrier = pltpu.get_barrier_semaphore()
    for o in range(1, depth):
        pl.semaphore_signal(barrier, inc=1, device_id=on_z(o), device_id_type=MESH)
    for o in range(1, side):
        pl.semaphore_signal(barrier, inc=1, device_id=on_x(o), device_id_type=MESH)
        pl.semaphore_signal(barrier, inc=1, device_id=on_y(o), device_id_type=MESH)
    pl.semaphore_signal(barrier, inc=1, device_id=sibling, device_id_type=MESH)

    def place_of(g, which):
        x_now = lax.rem(g + which, 2) == 0
        return x_now, jnp.where(x_now, my_x, my_y)

    def row_copy(it, g, which, o):
        buffer, send, recv = (r.first, r.first_send, r.first_recv) if which == 0 else (
            r.second, r.second_send, r.second_recv)
        x_now, me = place_of(g, which)
        (row, x_col), (_, y_col) = on_x(o), on_y(o)
        here = buffer.at[it, me, pl.ds(g * chunks, chunks)]
        return pltpu.make_async_remote_copy(
            src_ref=here, dst_ref=here, send_sem=send.at[it, g, o], recv_sem=recv.at[it, g, me],
            device_id=(row, jnp.where(x_now, x_col, y_col)), device_id_type=MESH)

    def row_arrived(it, g, which):
        buffer, recv = (r.first, r.first_recv) if which == 0 else (r.second, r.second_recv)
        _, me = place_of(g, which)
        for o in range(1, side):
            slot = lax.rem(me + o, side)
            here = buffer.at[it, slot, pl.ds(g * chunks, chunks)]
            pltpu.make_async_copy(here, here, recv.at[it, g, slot]).wait()

    def row_merged(it, g, which):
        buffer = r.first if which == 0 else r.second
        return merged_logs([buffer[it, d, pl.ds(g * chunks, chunks)] for d in range(side)])

    def pair_copy(it):
        return pltpu.make_async_remote_copy(
            src_ref=r.stage.at[it], dst_ref=r.pair.at[it, my_core],
            send_sem=r.pair_send.at[it], recv_sem=r.pair_recv.at[it],
            device_id=sibling, device_id_type=MESH)

    def ring_copy(it, o):
        here = r.ring.at[it, my_z]
        return pltpu.make_async_remote_copy(
            src_ref=here, dst_ref=here, send_sem=r.ring_send.at[it, o], recv_sem=r.ring_recv.at[it, my_z],
            device_id=on_z(o), device_id_type=MESH)

    def back_copy(it):
        here = r.gall.at[it, my_core]
        return pltpu.make_async_remote_copy(
            src_ref=here, dst_ref=here, send_sem=r.back_send.at[it], recv_sem=r.back_recv.at[it],
            device_id=sibling, device_id_type=MESH)

    @pl.loop(0, TGT_PARTS)
    def _(o):
        tgt_copy(o).wait()
        start_columns(r, o, tgt_part)

    for it in range(ITERS):
        @pl.loop(0, GROUPS)
        def _(g):
            if it == 0:
                src_copy(g).wait()
            _, me = place_of(g, 0)

            def place(c, value):
                r.first[it, me, c] = value

            row_group(r, it, g, chunks, place)
            if it == 0:
                @pl.when(g == 0)
                def _():
                    pl.semaphore_wait(barrier, 2 * (side - 1) + depth)

            for o in range(1, side):
                row_copy(it, g, 0, o).start()

        @pl.loop(0, GROUPS)
        def _(g):
            row_arrived(it, g, 0)
            _, me = place_of(g, 1)
            r.second[it, me, pl.ds(g * chunks, chunks)] = row_merged(it, g, 0)
            for o in range(1, side):
                row_copy(it, g, 1, o).start()
            if it == 0:
                make_group(r, g, chunks)

        @pl.loop(0, GROUPS)
        def _(g):
            row_arrived(it, g, 1)
            here = pl.ds(g * chunks, chunks)
            r.fall[here] = r.ls[here] * LOG2E - row_merged(it, g, 1)
            col_group(r, g, chunks)

        @pl.loop(0, half)
        def _(j):
            r.stage[it, j] = merge_columns(r, other * half + j)

        pair_copy(it).start()

        @pl.loop(0, half)
        def _(j):
            r.pair[it, my_core, j] = merge_columns(r, my_core * half + j)

        pair_copy(it).wait_recv()
        r.ring[it, my_z] = merged_logs([r.pair[it, 0], r.pair[it, 1]])
        far_first = sorted(range(1, depth), key=lambda o: -min(o, depth - o))
        for o in far_first:
            ring_copy(it, o).start()

        if it == 0:
            @pl.loop(0, n_col)
            def _(c):
                for t in range(TILES):
                    across = norms_across(r.src[TILES * c + t])
                    for h in range(2):
                        r.rnorm[c, pl.ds(2 * t + h, 1), :] = across[:, h * 128:(h + 1) * 128]

            @pl.loop(0, 2 * half)
            def _(c):
                for t in range(TILES):
                    across = norms_across(r.tgt[TILES * c + t])
                    for h in range(2):
                        r.cnorm[c, pl.ds(2 * t + h, 1), :] = across[:, h * 128:(h + 1) * 128]

        if it == ITERS - 1:
            r.f_out[...] = r.fall[...] * (1.0 / SCALE) + r.rnorm[...]

        @pl.loop(0, GROUPS)
        def _(g):
            for o in range(1, side):
                row_copy(it, g, 0, o).wait_send()
                row_copy(it, g, 1, o).wait_send()

        pair_copy(it).wait_send()

        for o in far_first:
            slot = lax.rem(my_z + o, depth)
            here = r.ring.at[it, slot]
            pltpu.make_async_copy(here, here, r.ring_recv.at[it, slot]).wait()
        r.gall[it, my_core] = (
            r.lt[pl.ds(my_core * half, half)] * LOG2E - merged_logs([r.ring[it, d] for d in range(depth)]))
        back_copy(it).start()

        def finish(core):
            if it < ITERS - 1:
                for j in range(half):
                    spread_columns(r, core * half + j, r.gall[it, core, j])
            else:
                here = pl.ds(core * half, half)
                r.g_out[here] = r.gall[it, core] * (1.0 / SCALE) + r.cnorm[here]

        finish(my_core)
        for o in far_first:
            ring_copy(it, o).wait_send()
        back_copy(it).wait()
        finish(other)


def handed_on(f_from, g_from, f_to, g_to):
    f_to[...] = f_from[...]
    g_to[...] = g_from[...]


def on_device(n_row, n_col, source, target, log_source, log_target, support, counts):
    row_count = support.shape[0]
    embed = source.shape[1]
    col_count = target.shape[0] // BS
    side = math.isqrt(n_col)
    depth = n_row // 2
    f32 = jnp.float32
    smem = pl.BlockSpec(memory_space=pltpu.SMEM)
    vmem = pl.BlockSpec(memory_space=pltpu.VMEM)
    hbm = pl.BlockSpec(memory_space=pl.ANY)
    dma = pltpu.SemaphoreType.DMA
    row_shape, col_shape = (row_count // TILES, 8, 128), (col_count // TILES, 8, 128)
    half_shape = (col_count // TILES // 2, 8, 128)
    gathered = TILES * 16 * row_count // (TILES * GROUPS)
    f, g = pl.pallas_call(
        functools.partial(kernel, n_row, n_col),
        out_shape=(jax.ShapeDtypeStruct(row_shape, f32), jax.ShapeDtypeStruct(col_shape, f32)),
        in_specs=[smem, smem, hbm, hbm, vmem, vmem],
        out_specs=(vmem, vmem),
        scratch_shapes=[
            pltpu.VMEM((row_count, BS, embed), jnp.bfloat16),
            pltpu.VMEM((col_count, BS, embed), jnp.bfloat16),
            pltpu.VMEM((row_count, BS, BS), f32),
            pltpu.VMEM((row_count, BS, BS), f32),
            pltpu.VMEM((col_count, BS, 128), f32),
            pltpu.VMEM((gathered, 128), f32),
            pltpu.VMEM((gathered, 128), f32),
            pltpu.VMEM(row_shape, jnp.int32),
            pltpu.VMEM(row_shape, f32),
            pltpu.VMEM(row_shape, f32),
            pltpu.VMEM(row_shape, f32),
            pltpu.VMEM(col_shape, f32),
            pltpu.VMEM((ITERS, side) + row_shape, f32),
            pltpu.VMEM((ITERS, side) + row_shape, f32),
            pltpu.VMEM((ITERS,) + half_shape, f32),
            pltpu.VMEM((ITERS, 2) + half_shape, f32),
            pltpu.VMEM((ITERS, depth) + half_shape, f32),
            pltpu.VMEM((ITERS, 2) + half_shape, f32),
            dma((TGT_PARTS,)),
            dma((GROUPS,)),
            dma((ITERS, GROUPS, side)), dma((ITERS, GROUPS, side)),
            dma((ITERS, GROUPS, side)), dma((ITERS, GROUPS, side)),
            dma((ITERS,)), dma((ITERS,)),
            dma((ITERS, depth)), dma((ITERS, depth)),
            dma((ITERS,)), dma((ITERS,)),
        ],
        compiler_params=pltpu.CompilerParams(
            collective_id=0, has_side_effects=True, vmem_limit_bytes=56 * 1024 * 1024),
    )(
        support.T, counts.T,
        source.reshape(row_count, BS, embed), target.reshape(col_count, BS, embed),
        log_source.reshape(row_shape), log_target.reshape(col_shape),
    )
    f, g = pl.pallas_call(
        handed_on,
        out_shape=(jax.ShapeDtypeStruct(row_shape, f32), jax.ShapeDtypeStruct(col_shape, f32)),
        in_specs=[vmem, vmem],
        out_specs=(vmem, vmem),
    )(f, g)
    return f.reshape(-1), g.reshape(-1)


def solution(mesh):
    placed = (P("row", None), P("col", None), P("row"), P("col"), P("row", "col"), P("row", "col"))
    body = functools.partial(on_device, mesh.shape["row"], mesh.shape["col"])
    return jax.shard_map(
        body, mesh=mesh, in_specs=placed, out_specs=(P("row"), P("col")), check_vma=False
    )
```

```python
import functools
import math

import jax
import jax.numpy as jnp
from jax import lax
from jax.experimental import pallas as pl
from jax.experimental.pallas import tpu as pltpu
from jax.sharding import PartitionSpec as P

BS = 256
ITERS = 2
entropic = 0.1
floor_value = -1e30
LOG2E = math.log2(math.e)
SCALE = LOG2E / entropic
MESH = pl.DeviceIdType.MESH
TILES = 4
GROUPS = 4
TGT_PARTS = 2
PART = 64


def dot_nt(a, b):
    return lax.dot_general(a, b, (((1,), (1,)), ((), ())), preferred_element_type=jnp.float32)


def lane_column(row):
    return jnp.transpose(jnp.broadcast_to(row, (128, 128)))


def tree(op, parts):
    parts = list(parts)
    while len(parts) > 1:
        paired = [op(a, b) for a, b in zip(parts[::2], parts[1::2])]
        parts = paired + parts[len(parts) - len(parts) % 2:]
    return parts[0]


def merged(pairs):
    peak = tree(jnp.maximum, [p for p, _ in pairs])
    return peak, tree(jnp.add, [s * jnp.exp2(p - peak) for p, s in pairs])


def log_sum(pair):
    return pair[0] + LOG2E * jnp.log(pair[1])


def merged_logs(parts):
    peak = tree(jnp.maximum, parts)
    return peak + LOG2E * jnp.log(tree(jnp.add, [jnp.exp2(part - peak) for part in parts]))


def tile_pairs(products, offsets):
    pairs = []
    for k in range(0, BS, PART):
        scores = (products(k) + offsets(k)).reshape(PART // 8, 8, 128)
        peak = jnp.max(scores, axis=0)
        pairs.append((peak, jnp.sum(jnp.exp2(scores - peak[None]), axis=0)))
    return merged(pairs)


def sublane_pairs(peaks, sums, count, stride):
    return merged([
        (peaks[pl.ds(s, count, stride=stride), :], sums[pl.ds(s, count, stride=stride), :])
        for s in range(stride)])


def squares(block):
    wide = block.astype(jnp.float32)
    return wide * wide


def norms_across(block):
    square = squares(block)
    high = square.astype(jnp.bfloat16)
    low = (square - high.astype(jnp.float32)).astype(jnp.bfloat16)
    ones = jnp.ones((8, block.shape[1]), jnp.bfloat16)
    return ((dot_nt(ones, high) + dot_nt(ones, low)) * (1.0 / block.shape[1]))[0:1]


def norm_chunks(blocks, norms, first):
    for c in (first, first + 1):
        for t in range(TILES):
            across = norms_across(blocks[TILES * c + t])
            for h in range(2):
                norms[c, pl.ds(2 * t + h, 1), :] = across[:, h * 128:(h + 1) * 128]


def block_of(r, i):
    return jnp.clip(r.sup[0, i] - r.first_block, 0, r.tgt.shape[0] - 1)


def start_columns(r, o, count):
    for a in range(count):
        block = r.tgt[count * o + a]
        down = jnp.sum(squares(block), axis=1, keepdims=True) * (-SCALE / block.shape[1])
        r.gcol[count * o + a] = jnp.broadcast_to(down, (BS, 128))


def row_group(r, it, g, chunks, place):
    for k in range(chunks):
        c = chunks * g + k
        for t in range(TILES):
            i = TILES * c + t
            block = block_of(r, i)
            dead = jnp.where(r.cnt[0, i] > 0, 0.0, floor_value)
            if it == 0:
                made = dot_nt(r.tgt[block], r.src[i]) * (2.0 * SCALE / r.src.shape[2])
                r.dots_qp[i] = made
            for h in range(2):
                lanes = slice(h * 128, (h + 1) * 128)
                if it == 0:
                    products = lambda k: made[k:k + PART, lanes]
                else:
                    products = lambda k: r.dots_qp[i, k:k + PART, lanes]
                peak, total = tile_pairs(products, lambda k: r.gcol[block, k:k + PART, :])
                here = pl.ds(64 * k + 8 * (2 * t + h), 8)
                r.peaks[here, :] = peak + dead
                r.sums[here, :] = total
        at = pl.ds(64 * k, 64)
        place(c, log_sum(sublane_pairs(r.peaks.at[at], r.sums.at[at], 8, 8)))


def make_group(r, g, chunks):
    sublane = lax.broadcasted_iota(jnp.int32, (8, 128), 0)
    for k in range(chunks):
        c = chunks * g + k
        names = jnp.full((8, 128), -1, jnp.int32)
        for t in range(TILES):
            i = TILES * c + t
            block = block_of(r, i)
            r.dots_pq[i] = dot_nt(r.src[i], r.tgt[block]) * (2.0 * SCALE / r.src.shape[2])
            name = jnp.where(r.cnt[0, i] > 0, block, -1)
            names = jnp.where(lax.rem(sublane, TILES) == t, name, names)
        r.key[c] = names


def col_group(r, g, chunks):
    for k in range(chunks):
        c = chunks * g + k
        for t in range(TILES):
            i = TILES * c + t
            down = [lane_column(r.fall[c, pl.ds(2 * t + h, 1), :]) for h in range(2)]
            for h in range(2):
                peak, total = tile_pairs(
                    lambda k: r.dots_pq[i, k:k + PART, h * 128:(h + 1) * 128],
                    lambda k: down[k // 128][k % 128:k % 128 + PART])
                here = pl.ds(64 * k + 8 * (TILES * h + t), 8)
                r.peaks[here, :] = peak
                r.sums[here, :] = total
        at = pl.ds(64 * k, 64)
        r.lpart[c] = log_sum(sublane_pairs(r.peaks.at[at], r.sums.at[at], 8, 8))


def merge_columns(r, chunk):
    for u in range(4):
        mine = jnp.where(r.key[...] == 4 * chunk + u, r.lpart[...], floor_value)
        peak = jnp.max(mine, axis=0)
        here = pl.ds(8 * u, 8)
        r.peaks[here, :] = peak
        r.sums[here, :] = jnp.sum(jnp.exp2(mine - peak[None]), axis=0)
    return log_sum(sublane_pairs(r.peaks, r.sums, 8, 4))


def spread_columns(r, chunk, rows):
    for j in range(8):
        r.gcol[4 * chunk + j // 2, (j % 2) * 128:(j % 2 + 1) * 128, :] = lane_column(rows[j:j + 1])


REFS = (
    "sup", "cnt", "src_hbm", "tgt_hbm", "ls", "lt", "f_out", "g_out", "src", "tgt", "dots_qp", "dots_pq",
    "gcol", "peaks", "sums", "key", "fall", "lpart", "rnorm", "cnorm", "first", "second", "stage", "pair",
    "ring", "gall", "tgt_sem", "src_sem", "first_send", "first_recv", "second_send", "second_recv",
    "pair_send", "pair_recv", "ring_send", "ring_recv", "back_send", "back_recv",
)


class Refs:
    pass


def kernel(n_row, n_col, *refs):
    r = Refs()
    for name, ref in zip(REFS, refs, strict=True):
        setattr(r, name, ref)
    side = math.isqrt(n_col)
    depth = n_row // 2
    my_row, my_col = lax.axis_index("row"), lax.axis_index("col")
    my_x, my_y = my_col // side, lax.rem(my_col, side)
    my_z, my_core = my_row // 2, lax.rem(my_row, 2)
    other = 1 - my_core
    r.first_block = my_col * r.tgt.shape[0]
    chunks = n_col // GROUPS
    half = r.gall.shape[2]

    tgt_part = r.tgt.shape[0] // TGT_PARTS

    def tgt_copy(o):
        here = pl.ds(o * tgt_part, tgt_part)
        return pltpu.make_async_copy(r.tgt_hbm.at[here], r.tgt.at[here], r.tgt_sem.at[o])

    for o in range(TGT_PARTS):
        tgt_copy(o).start()

    def src_copy(g):
        here = pl.ds(g * chunks * TILES, chunks * TILES)
        return pltpu.make_async_copy(r.src_hbm.at[here], r.src.at[here], r.src_sem.at[g])

    for g in range(GROUPS):
        src_copy(g).start()

    def on_x(o):
        return (my_row, lax.rem(my_x + o, side) * side + my_y)

    def on_y(o):
        return (my_row, my_x * side + lax.rem(my_y + o, side))

    def on_z(o):
        return (lax.rem(my_z + o, depth) * 2 + my_core, my_col)

    sibling = (my_z * 2 + other, my_col)
    barrier = pltpu.get_barrier_semaphore()
    for o in range(1, depth):
        pl.semaphore_signal(barrier, inc=1, device_id=on_z(o), device_id_type=MESH)
    for o in range(1, side):
        pl.semaphore_signal(barrier, inc=1, device_id=on_x(o), device_id_type=MESH)
        pl.semaphore_signal(barrier, inc=1, device_id=on_y(o), device_id_type=MESH)
    pl.semaphore_signal(barrier, inc=1, device_id=sibling, device_id_type=MESH)

    def place_of(g, which):
        x_now = lax.rem(g + which, 2) == 0
        return x_now, jnp.where(x_now, my_x, my_y)

    def row_copy(it, g, which, o):
        buffer, send, recv = (r.first, r.first_send, r.first_recv) if which == 0 else (
            r.second, r.second_send, r.second_recv)
        x_now, me = place_of(g, which)
        (row, x_col), (_, y_col) = on_x(o), on_y(o)
        here = buffer.at[it, me, pl.ds(g * chunks, chunks)]
        return pltpu.make_async_remote_copy(
            src_ref=here, dst_ref=here, send_sem=send.at[it, g, o], recv_sem=recv.at[it, g, me],
            device_id=(row, jnp.where(x_now, x_col, y_col)), device_id_type=MESH)

    def row_arrived(it, g, which):
        buffer, recv = (r.first, r.first_recv) if which == 0 else (r.second, r.second_recv)
        _, me = place_of(g, which)
        for o in range(1, side):
            slot = lax.rem(me + o, side)
            here = buffer.at[it, slot, pl.ds(g * chunks, chunks)]
            pltpu.make_async_copy(here, here, recv.at[it, g, slot]).wait()

    def row_merged(it, g, which):
        buffer = r.first if which == 0 else r.second
        return merged_logs([buffer[it, d, pl.ds(g * chunks, chunks)] for d in range(side)])

    def pair_copy(it):
        return pltpu.make_async_remote_copy(
            src_ref=r.stage.at[it], dst_ref=r.pair.at[it, my_core],
            send_sem=r.pair_send.at[it], recv_sem=r.pair_recv.at[it],
            device_id=sibling, device_id_type=MESH)

    def ring_copy(it, o):
        here = r.ring.at[it, my_z]
        return pltpu.make_async_remote_copy(
            src_ref=here, dst_ref=here, send_sem=r.ring_send.at[it, o], recv_sem=r.ring_recv.at[it, my_z],
            device_id=on_z(o), device_id_type=MESH)

    def back_copy(it):
        here = r.gall.at[it, my_core]
        return pltpu.make_async_remote_copy(
            src_ref=here, dst_ref=here, send_sem=r.back_send.at[it], recv_sem=r.back_recv.at[it],
            device_id=sibling, device_id_type=MESH)

    @pl.loop(0, TGT_PARTS)
    def _(o):
        tgt_copy(o).wait()
        start_columns(r, o, tgt_part)

    for it in range(ITERS):
        @pl.loop(0, GROUPS)
        def _(g):
            if it == 0:
                src_copy(g).wait()
            _, me = place_of(g, 0)

            def place(c, value):
                r.first[it, me, c] = value

            row_group(r, it, g, chunks, place)
            if it == 0:
                @pl.when(g == 0)
                def _():
                    pl.semaphore_wait(barrier, 2 * (side - 1) + depth)

            for o in range(1, side):
                row_copy(it, g, 0, o).start()

        @pl.loop(0, GROUPS)
        def _(g):
            row_arrived(it, g, 0)
            _, me = place_of(g, 1)
            r.second[it, me, pl.ds(g * chunks, chunks)] = row_merged(it, g, 0)
            for o in range(1, side):
                row_copy(it, g, 1, o).start()
            if it == 0:
                make_group(r, g, chunks)

        @pl.loop(0, GROUPS)
        def _(g):
            row_arrived(it, g, 1)
            here = pl.ds(g * chunks, chunks)
            r.fall[here] = r.ls[here] * LOG2E - row_merged(it, g, 1)
            col_group(r, g, chunks)

        @pl.loop(0, half)
        def _(j):
            r.stage[it, j] = merge_columns(r, other * half + j)

        pair_copy(it).start()

        @pl.loop(0, half)
        def _(j):
            r.pair[it, my_core, j] = merge_columns(r, my_core * half + j)

        pair_copy(it).wait_recv()
        r.ring[it, my_z] = merged_logs([r.pair[it, 0], r.pair[it, 1]])
        far_first = sorted(range(1, depth), key=lambda o: -min(o, depth - o))
        for o in far_first:
            ring_copy(it, o).start()

        if it == 0:
            pl.loop(0, half)(lambda c: norm_chunks(r.tgt, r.cnorm, 2 * c))

        if it == ITERS - 1:
            pl.loop(0, n_col // 2)(lambda c: norm_chunks(r.src, r.rnorm, 2 * c))
            r.f_out[...] = r.fall[...] * (1.0 / SCALE) + r.rnorm[...]

        @pl.loop(0, GROUPS)
        def _(g):
            for o in range(1, side):
                row_copy(it, g, 0, o).wait_send()
                row_copy(it, g, 1, o).wait_send()

        pair_copy(it).wait_send()

        for o in far_first:
            slot = lax.rem(my_z + o, depth)
            here = r.ring.at[it, slot]
            pltpu.make_async_copy(here, here, r.ring_recv.at[it, slot]).wait()
        r.gall[it, my_core] = (
            r.lt[pl.ds(my_core * half, half)] * LOG2E - merged_logs([r.ring[it, d] for d in range(depth)]))
        back_copy(it).start()

        def finish(core):
            if it < ITERS - 1:
                for j in range(half):
                    spread_columns(r, core * half + j, r.gall[it, core, j])
            else:
                here = pl.ds(core * half, half)
                r.g_out[here] = r.gall[it, core] * (1.0 / SCALE) + r.cnorm[here]

        finish(my_core)
        for o in far_first:
            ring_copy(it, o).wait_send()
        back_copy(it).wait()
        finish(other)


def handed_on(f_from, g_from, f_to, g_to):
    f_to[...] = f_from[...]
    g_to[...] = g_from[...]


def on_device(n_row, n_col, source, target, log_source, log_target, support, counts):
    row_count = support.shape[0]
    embed = source.shape[1]
    col_count = target.shape[0] // BS
    side = math.isqrt(n_col)
    depth = n_row // 2
    f32 = jnp.float32
    smem = pl.BlockSpec(memory_space=pltpu.SMEM)
    vmem = pl.BlockSpec(memory_space=pltpu.VMEM)
    hbm = pl.BlockSpec(memory_space=pl.ANY)
    dma = pltpu.SemaphoreType.DMA
    row_shape, col_shape = (row_count // TILES, 8, 128), (col_count // TILES, 8, 128)
    half_shape = (col_count // TILES // 2, 8, 128)
    gathered = TILES * 16 * row_count // (TILES * GROUPS)
    f, g = pl.pallas_call(
        functools.partial(kernel, n_row, n_col),
        out_shape=(jax.ShapeDtypeStruct(row_shape, f32), jax.ShapeDtypeStruct(col_shape, f32)),
        in_specs=[smem, smem, hbm, hbm, vmem, vmem],
        out_specs=(vmem, vmem),
        scratch_shapes=[
            pltpu.VMEM((row_count, BS, embed), jnp.bfloat16),
            pltpu.VMEM((col_count, BS, embed), jnp.bfloat16),
            pltpu.VMEM((row_count, BS, BS), f32),
            pltpu.VMEM((row_count, BS, BS), f32),
            pltpu.VMEM((col_count, BS, 128), f32),
            pltpu.VMEM((gathered, 128), f32),
            pltpu.VMEM((gathered, 128), f32),
            pltpu.VMEM(row_shape, jnp.int32),
            pltpu.VMEM(row_shape, f32),
            pltpu.VMEM(row_shape, f32),
            pltpu.VMEM(row_shape, f32),
            pltpu.VMEM(col_shape, f32),
            pltpu.VMEM((ITERS, side) + row_shape, f32),
            pltpu.VMEM((ITERS, side) + row_shape, f32),
            pltpu.VMEM((ITERS,) + half_shape, f32),
            pltpu.VMEM((ITERS, 2) + half_shape, f32),
            pltpu.VMEM((ITERS, depth) + half_shape, f32),
            pltpu.VMEM((ITERS, 2) + half_shape, f32),
            dma((TGT_PARTS,)),
            dma((GROUPS,)),
            dma((ITERS, GROUPS, side)), dma((ITERS, GROUPS, side)),
            dma((ITERS, GROUPS, side)), dma((ITERS, GROUPS, side)),
            dma((ITERS,)), dma((ITERS,)),
            dma((ITERS, depth)), dma((ITERS, depth)),
            dma((ITERS,)), dma((ITERS,)),
        ],
        compiler_params=pltpu.CompilerParams(
            collective_id=0, has_side_effects=True, vmem_limit_bytes=56 * 1024 * 1024),
    )(
        support.T, counts.T,
        source.reshape(row_count, BS, embed), target.reshape(col_count, BS, embed),
        log_source.reshape(row_shape), log_target.reshape(col_shape),
    )
    f, g = pl.pallas_call(
        handed_on,
        out_shape=(jax.ShapeDtypeStruct(row_shape, f32), jax.ShapeDtypeStruct(col_shape, f32)),
        in_specs=[vmem, vmem],
        out_specs=(vmem, vmem),
    )(f, g)
    return f.reshape(-1), g.reshape(-1)


def solution(mesh):
    placed = (P("row", None), P("col", None), P("row"), P("col"), P("row", "col"), P("row", "col"))
    body = functools.partial(on_device, mesh.shape["row"], mesh.shape["col"])
    return jax.shard_map(
        body, mesh=mesh, in_specs=placed, out_specs=(P("row"), P("col")), check_vma=False
    )
```

```python
import functools
import math

import jax
import jax.numpy as jnp
from jax import lax
from jax.experimental import pallas as pl
from jax.experimental.pallas import tpu as pltpu
from jax.sharding import PartitionSpec as P

BS = 256
ITERS = 2
entropic = 0.1
floor_value = -1e30
LOG2E = math.log2(math.e)
SCALE = LOG2E / entropic
MESH = pl.DeviceIdType.MESH
TILES = 4
GROUPS = 4
TGT_PARTS = 2
PART = 64


def dot_nt(a, b):
    return lax.dot_general(a, b, (((1,), (1,)), ((), ())), preferred_element_type=jnp.float32)


def lane_column(row):
    return jnp.transpose(jnp.broadcast_to(row, (128, 128)))


def tree(op, parts):
    parts = list(parts)
    while len(parts) > 1:
        paired = [op(a, b) for a, b in zip(parts[::2], parts[1::2])]
        parts = paired + parts[len(parts) - len(parts) % 2:]
    return parts[0]


def merged(pairs):
    peak = tree(jnp.maximum, [p for p, _ in pairs])
    return peak, tree(jnp.add, [s * jnp.exp2(p - peak) for p, s in pairs])


def log_sum(pair):
    return pair[0] + LOG2E * jnp.log(pair[1])


def merged_logs(parts):
    peak = tree(jnp.maximum, parts)
    return peak + LOG2E * jnp.log(tree(jnp.add, [jnp.exp2(part - peak) for part in parts]))


def tile_pairs(products, offsets):
    pairs = []
    for k in range(0, BS, PART):
        scores = (products(k) + offsets(k)).reshape(PART // 8, 8, 128)
        peak = jnp.max(scores, axis=0)
        pairs.append((peak, jnp.sum(jnp.exp2(scores - peak[None]), axis=0)))
    return merged(pairs)


def sublane_pairs(peaks, sums, count, stride):
    return merged([
        (peaks[pl.ds(s, count, stride=stride), :], sums[pl.ds(s, count, stride=stride), :])
        for s in range(stride)])


def squares(block):
    wide = block.astype(jnp.float32)
    return wide * wide


def norms_across(block):
    square = squares(block)
    high = square.astype(jnp.bfloat16)
    low = (square - high.astype(jnp.float32)).astype(jnp.bfloat16)
    ones = jnp.ones((8, block.shape[1]), jnp.bfloat16)
    return ((dot_nt(ones, high) + dot_nt(ones, low)) * (1.0 / block.shape[1]))[0:1]


def norm_chunks(blocks, norms, first):
    for c in (first, first + 1):
        for t in range(TILES):
            across = norms_across(blocks[TILES * c + t])
            for h in range(2):
                norms[c, pl.ds(2 * t + h, 1), :] = across[:, h * 128:(h + 1) * 128]


def block_of(r, i):
    return jnp.clip(r.sup[0, i] - r.first_block, 0, r.tgt.shape[0] - 1)


def start_columns(r, o, count):
    for a in range(count):
        block = r.tgt[count * o + a]
        down = jnp.sum(squares(block), axis=1, keepdims=True) * (-SCALE / block.shape[1])
        r.gcol[count * o + a] = jnp.broadcast_to(down, (BS, 128))


def row_group(r, it, g, chunks, place):
    for k in range(chunks):
        c = chunks * g + k
        for t in range(TILES):
            i = TILES * c + t
            block = block_of(r, i)
            dead = jnp.where(r.cnt[0, i] > 0, 0.0, floor_value)
            if it == 0:
                made = dot_nt(r.tgt[block], r.src[i]) * (2.0 * SCALE / r.src.shape[2])
                r.dots_qp[i] = made
            for h in range(2):
                lanes = slice(h * 128, (h + 1) * 128)
                if it == 0:
                    products = lambda k: made[k:k + PART, lanes]
                else:
                    products = lambda k: r.dots_qp[i, k:k + PART, lanes]
                peak, total = tile_pairs(products, lambda k: r.gcol[block, k:k + PART, :])
                here = pl.ds(64 * k + 8 * (2 * t + h), 8)
                r.peaks[here, :] = peak + dead
                r.sums[here, :] = total
        at = pl.ds(64 * k, 64)
        place(c, log_sum(sublane_pairs(r.peaks.at[at], r.sums.at[at], 8, 8)))


def make_group(r, g, chunks):
    sublane = lax.broadcasted_iota(jnp.int32, (8, 128), 0)
    for k in range(chunks):
        c = chunks * g + k
        names = jnp.full((8, 128), -1, jnp.int32)
        for t in range(TILES):
            i = TILES * c + t
            block = block_of(r, i)
            r.dots_pq[i] = dot_nt(r.src[i], r.tgt[block]) * (2.0 * SCALE / r.src.shape[2])
            name = jnp.where(r.cnt[0, i] > 0, block, -1)
            names = jnp.where(lax.rem(sublane, TILES) == t, name, names)
        r.key[c] = names


def col_group(r, g, chunks):
    for k in range(chunks):
        c = chunks * g + k
        for t in range(TILES):
            i = TILES * c + t
            down = [lane_column(r.fall[c, pl.ds(2 * t + h, 1), :]) for h in range(2)]
            for h in range(2):
                peak, total = tile_pairs(
                    lambda k: r.dots_pq[i, k:k + PART, h * 128:(h + 1) * 128],
                    lambda k: down[k // 128][k % 128:k % 128 + PART])
                here = pl.ds(64 * k + 8 * (TILES * h + t), 8)
                r.peaks[here, :] = peak
                r.sums[here, :] = total
        at = pl.ds(64 * k, 64)
        r.lpart[c] = log_sum(sublane_pairs(r.peaks.at[at], r.sums.at[at], 8, 8))


def merge_columns(r, chunk, slot):
    for u in range(4):
        mine = jnp.where(r.key[...] == 4 * chunk + u, r.lpart[...], floor_value)
        peak = jnp.max(mine, axis=0)
        here = pl.ds(32 * slot + 8 * u, 8)
        r.peaks[here, :] = peak
        r.sums[here, :] = jnp.sum(jnp.exp2(mine - peak[None]), axis=0)
    at = pl.ds(32 * slot, 32)
    return log_sum(sublane_pairs(r.peaks.at[at], r.sums.at[at], 8, 4))


def spread_columns(r, chunk, rows):
    for j in range(8):
        r.gcol[4 * chunk + j // 2, (j % 2) * 128:(j % 2 + 1) * 128, :] = lane_column(rows[j:j + 1])


REFS = (
    "sup_hbm", "cnt_hbm", "src_hbm", "tgt_hbm", "ls_hbm", "lt_hbm", "f_out", "g_out", "sup", "cnt", "ls",
    "lt", "src", "tgt", "dots_qp", "dots_pq", "gcol", "peaks", "sums", "key", "fall", "lpart", "rnorm",
    "cnorm", "first", "second", "stage", "pair", "ring", "gall", "tgt_sem", "src_sem", "slot_sem",
    "weight_sem", "first_send", "first_recv", "second_send", "second_recv", "pair_send", "pair_recv",
    "ring_send", "ring_recv", "back_send", "back_recv",
)


class Refs:
    pass


def kernel(n_row, n_col, *refs):
    r = Refs()
    for name, ref in zip(REFS, refs, strict=True):
        setattr(r, name, ref)
    side = math.isqrt(n_col)
    depth = n_row // 2
    my_row, my_col = lax.axis_index("row"), lax.axis_index("col")
    my_x, my_y = my_col // side, lax.rem(my_col, side)
    my_z, my_core = my_row // 2, lax.rem(my_row, 2)
    other = 1 - my_core
    r.first_block = my_col * r.tgt.shape[0]
    chunks = n_col // GROUPS
    half = r.gall.shape[2]

    tgt_part = r.tgt.shape[0] // TGT_PARTS

    def tgt_copy(o):
        here = pl.ds(o * tgt_part, tgt_part)
        return pltpu.make_async_copy(r.tgt_hbm.at[here], r.tgt.at[here], r.tgt_sem.at[o])

    for o in range(TGT_PARTS):
        tgt_copy(o).start()

    slot_copies = [
        pltpu.make_async_copy(r.sup_hbm, r.sup, r.slot_sem.at[0]),
        pltpu.make_async_copy(r.cnt_hbm, r.cnt, r.slot_sem.at[1])]
    for copy in slot_copies:
        copy.start()

    def src_copy(g):
        here = pl.ds(g * chunks * TILES, chunks * TILES)
        return pltpu.make_async_copy(r.src_hbm.at[here], r.src.at[here], r.src_sem.at[g])

    for g in range(GROUPS):
        src_copy(g).start()

    weight_copies = [
        pltpu.make_async_copy(r.ls_hbm, r.ls, r.weight_sem.at[0]),
        pltpu.make_async_copy(r.lt_hbm, r.lt, r.weight_sem.at[1])]
    for copy in weight_copies:
        copy.start()

    def on_x(o):
        return (my_row, lax.rem(my_x + o, side) * side + my_y)

    def on_y(o):
        return (my_row, my_x * side + lax.rem(my_y + o, side))

    def on_z(o):
        return (lax.rem(my_z + o, depth) * 2 + my_core, my_col)

    sibling = (my_z * 2 + other, my_col)
    barrier = pltpu.get_barrier_semaphore()
    for o in range(1, depth):
        pl.semaphore_signal(barrier, inc=1, device_id=on_z(o), device_id_type=MESH)
    for o in range(1, side):
        pl.semaphore_signal(barrier, inc=1, device_id=on_x(o), device_id_type=MESH)
        pl.semaphore_signal(barrier, inc=1, device_id=on_y(o), device_id_type=MESH)
    pl.semaphore_signal(barrier, inc=1, device_id=sibling, device_id_type=MESH)

    def place_of(g, which):
        x_now = lax.rem(g + which, 2) == 0
        return x_now, jnp.where(x_now, my_x, my_y)

    def row_copy(it, g, which, o):
        buffer, send, recv = (r.first, r.first_send, r.first_recv) if which == 0 else (
            r.second, r.second_send, r.second_recv)
        x_now, me = place_of(g, which)
        (row, x_col), (_, y_col) = on_x(o), on_y(o)
        here = buffer.at[it, me, pl.ds(g * chunks, chunks)]
        return pltpu.make_async_remote_copy(
            src_ref=here, dst_ref=here, send_sem=send.at[it, g, o], recv_sem=recv.at[it, g, me],
            device_id=(row, jnp.where(x_now, x_col, y_col)), device_id_type=MESH)

    def row_arrived(it, g, which):
        buffer, recv = (r.first, r.first_recv) if which == 0 else (r.second, r.second_recv)
        _, me = place_of(g, which)
        for o in range(1, side):
            slot = lax.rem(me + o, side)
            here = buffer.at[it, slot, pl.ds(g * chunks, chunks)]
            pltpu.make_async_copy(here, here, recv.at[it, g, slot]).wait()

    def row_merged(it, g, which):
        buffer = r.first if which == 0 else r.second
        return merged_logs([buffer[it, d, pl.ds(g * chunks, chunks)] for d in range(side)])

    def pair_copy(it):
        return pltpu.make_async_remote_copy(
            src_ref=r.stage.at[it], dst_ref=r.pair.at[it, my_core],
            send_sem=r.pair_send.at[it], recv_sem=r.pair_recv.at[it],
            device_id=sibling, device_id_type=MESH)

    def ring_copy(it, o):
        here = r.ring.at[it, my_z]
        return pltpu.make_async_remote_copy(
            src_ref=here, dst_ref=here, send_sem=r.ring_send.at[it, o], recv_sem=r.ring_recv.at[it, my_z],
            device_id=on_z(o), device_id_type=MESH)

    def back_copy(it):
        here = r.gall.at[it, my_core]
        return pltpu.make_async_remote_copy(
            src_ref=here, dst_ref=here, send_sem=r.back_send.at[it], recv_sem=r.back_recv.at[it],
            device_id=sibling, device_id_type=MESH)

    @pl.loop(0, TGT_PARTS)
    def _(o):
        tgt_copy(o).wait()
        start_columns(r, o, tgt_part)

    for copy in slot_copies:
        copy.wait()

    for it in range(ITERS):
        @pl.loop(0, GROUPS)
        def _(g):
            if it == 0:
                src_copy(g).wait()
            _, me = place_of(g, 0)

            def place(c, value):
                r.first[it, me, c] = value

            row_group(r, it, g, chunks, place)
            if it == 0:
                @pl.when(g == 0)
                def _():
                    pl.semaphore_wait(barrier, 2 * (side - 1) + depth)

            for o in range(1, side):
                row_copy(it, g, 0, o).start()

        @pl.loop(0, GROUPS)
        def _(g):
            if it == 0:
                @pl.when(g == 0)
                def _():
                    for copy in weight_copies:
                        copy.wait()

            row_arrived(it, g, 0)
            _, me = place_of(g, 1)
            r.second[it, me, pl.ds(g * chunks, chunks)] = row_merged(it, g, 0)
            for o in range(1, side):
                row_copy(it, g, 1, o).start()
            if it == 0:
                make_group(r, g, chunks)

        @pl.loop(0, GROUPS)
        def _(g):
            row_arrived(it, g, 1)
            here = pl.ds(g * chunks, chunks)
            r.fall[here] = r.ls[here] * LOG2E - row_merged(it, g, 1)
            col_group(r, g, chunks)

        for j in range(half):
            r.stage[it, j] = merge_columns(r, other * half + j, j)

        pair_copy(it).start()

        for j in range(half):
            r.pair[it, my_core, j] = merge_columns(r, my_core * half + j, j)

        pair_copy(it).wait_recv()
        r.ring[it, my_z] = merged_logs([r.pair[it, 0], r.pair[it, 1]])
        far_first = sorted(range(1, depth), key=lambda o: -min(o, depth - o))
        for o in far_first:
            ring_copy(it, o).start()

        if it == 0:
            pl.loop(0, half)(lambda c: norm_chunks(r.tgt, r.cnorm, 2 * c))

        if it == ITERS - 1:
            pl.loop(0, n_col // 2)(lambda c: norm_chunks(r.src, r.rnorm, 2 * c))
            r.f_out[...] = r.fall[...] * (1.0 / SCALE) + r.rnorm[...]

        @pl.loop(0, GROUPS)
        def _(g):
            for o in range(1, side):
                row_copy(it, g, 0, o).wait_send()
                row_copy(it, g, 1, o).wait_send()

        pair_copy(it).wait_send()

        for o in far_first:
            slot = lax.rem(my_z + o, depth)
            here = r.ring.at[it, slot]
            pltpu.make_async_copy(here, here, r.ring_recv.at[it, slot]).wait()
        r.gall[it, my_core] = (
            r.lt[pl.ds(my_core * half, half)] * LOG2E - merged_logs([r.ring[it, d] for d in range(depth)]))
        back_copy(it).start()

        def finish(core):
            if it < ITERS - 1:
                for j in range(half):
                    spread_columns(r, core * half + j, r.gall[it, core, j])
            else:
                here = pl.ds(core * half, half)
                r.g_out[here] = r.gall[it, core] * (1.0 / SCALE) + r.cnorm[here]

        finish(my_core)
        for o in far_first:
            ring_copy(it, o).wait_send()
        back_copy(it).wait()
        finish(other)


def handed_on(f_from, g_from, f_to, g_to):
    f_to[...] = f_from[...]
    g_to[...] = g_from[...]


def on_device(n_row, n_col, source, target, log_source, log_target, support, counts):
    row_count = support.shape[0]
    embed = source.shape[1]
    col_count = target.shape[0] // BS
    side = math.isqrt(n_col)
    depth = n_row // 2
    f32 = jnp.float32
    vmem = pl.BlockSpec(memory_space=pltpu.VMEM)
    hbm = pl.BlockSpec(memory_space=pl.ANY)
    dma = pltpu.SemaphoreType.DMA
    row_shape, col_shape = (row_count // TILES, 8, 128), (col_count // TILES, 8, 128)
    half_shape = (col_count // TILES // 2, 8, 128)
    gathered = TILES * 16 * row_count // (TILES * GROUPS)
    f, g = pl.pallas_call(
        functools.partial(kernel, n_row, n_col),
        out_shape=(jax.ShapeDtypeStruct(row_shape, f32), jax.ShapeDtypeStruct(col_shape, f32)),
        in_specs=[hbm] * 6,
        out_specs=(vmem, vmem),
        scratch_shapes=[
            pltpu.SMEM((1, row_count), jnp.int32),
            pltpu.SMEM((1, row_count), jnp.int32),
            pltpu.VMEM(row_shape, f32),
            pltpu.VMEM(col_shape, f32),
            pltpu.VMEM((row_count, BS, embed), jnp.bfloat16),
            pltpu.VMEM((col_count, BS, embed), jnp.bfloat16),
            pltpu.VMEM((row_count, BS, BS), f32),
            pltpu.VMEM((row_count, BS, BS), f32),
            pltpu.VMEM((col_count, BS, 128), f32),
            pltpu.VMEM((gathered, 128), f32),
            pltpu.VMEM((gathered, 128), f32),
            pltpu.VMEM(row_shape, jnp.int32),
            pltpu.VMEM(row_shape, f32),
            pltpu.VMEM(row_shape, f32),
            pltpu.VMEM(row_shape, f32),
            pltpu.VMEM(col_shape, f32),
            pltpu.VMEM((ITERS, side) + row_shape, f32),
            pltpu.VMEM((ITERS, side) + row_shape, f32),
            pltpu.VMEM((ITERS,) + half_shape, f32),
            pltpu.VMEM((ITERS, 2) + half_shape, f32),
            pltpu.VMEM((ITERS, depth) + half_shape, f32),
            pltpu.VMEM((ITERS, 2) + half_shape, f32),
            dma((TGT_PARTS,)),
            dma((GROUPS,)),
            dma((2,)),
            dma((2,)),
            dma((ITERS, GROUPS, side)), dma((ITERS, GROUPS, side)),
            dma((ITERS, GROUPS, side)), dma((ITERS, GROUPS, side)),
            dma((ITERS,)), dma((ITERS,)),
            dma((ITERS, depth)), dma((ITERS, depth)),
            dma((ITERS,)), dma((ITERS,)),
        ],
        compiler_params=pltpu.CompilerParams(
            collective_id=0, has_side_effects=True, vmem_limit_bytes=56 * 1024 * 1024),
    )(
        support.T, counts.T,
        source.reshape(row_count, BS, embed), target.reshape(col_count, BS, embed),
        log_source.reshape(row_shape), log_target.reshape(col_shape),
    )
    f, g = pl.pallas_call(
        handed_on,
        out_shape=(jax.ShapeDtypeStruct(row_shape, f32), jax.ShapeDtypeStruct(col_shape, f32)),
        in_specs=[vmem, vmem],
        out_specs=(vmem, vmem),
    )(f, g)
    return f.reshape(-1), g.reshape(-1)


def solution(mesh):
    placed = (P("row", None), P("col", None), P("row"), P("col"), P("row", "col"), P("row", "col"))
    body = functools.partial(on_device, mesh.shape["row"], mesh.shape["col"])
    return jax.shard_map(
        body, mesh=mesh, in_specs=placed, out_specs=(P("row"), P("col")), check_vma=False
    )
```

```python
import functools
import math

import jax
import jax.numpy as jnp
from jax import lax
from jax.experimental import pallas as pl
from jax.experimental.pallas import tpu as pltpu
from jax.sharding import PartitionSpec as P

BS = 256
ITERS = 2
entropic = 0.1
floor_value = -1e30
LOG2E = math.log2(math.e)
SCALE = LOG2E / entropic
MESH = pl.DeviceIdType.MESH
TILES = 4
GROUPS = 4
TGT_PARTS = 2
PART = 64


def dot_nt(a, b):
    return lax.dot_general(a, b, (((1,), (1,)), ((), ())), preferred_element_type=jnp.float32)


def lane_column(row):
    return jnp.transpose(jnp.broadcast_to(row, (128, 128)))


def tree(op, parts):
    parts = list(parts)
    while len(parts) > 1:
        paired = [op(a, b) for a, b in zip(parts[::2], parts[1::2])]
        parts = paired + parts[len(parts) - len(parts) % 2:]
    return parts[0]


def merged(pairs):
    peak = tree(jnp.maximum, [p for p, _ in pairs])
    return peak, tree(jnp.add, [s * jnp.exp2(p - peak) for p, s in pairs])


def log_sum(pair):
    return pair[0] + LOG2E * jnp.log(pair[1])


def merged_logs(parts):
    peak = tree(jnp.maximum, parts)
    return peak + LOG2E * jnp.log(tree(jnp.add, [jnp.exp2(part - peak) for part in parts]))


def tile_pairs(products, offsets):
    pairs = []
    for k in range(0, BS, PART):
        scores = (products(k) + offsets(k)).reshape(PART // 8, 8, 128)
        peak = jnp.max(scores, axis=0)
        pairs.append((peak, jnp.sum(jnp.exp2(scores - peak[None]), axis=0)))
    return merged(pairs)


def sublane_pairs(peaks, sums, count, stride):
    return merged([
        (peaks[pl.ds(s, count, stride=stride), :], sums[pl.ds(s, count, stride=stride), :])
        for s in range(stride)])


def squares(block):
    wide = block.astype(jnp.float32)
    return wide * wide


def norms_across(block):
    square = squares(block)
    high = square.astype(jnp.bfloat16)
    low = (square - high.astype(jnp.float32)).astype(jnp.bfloat16)
    ones = jnp.ones((8, block.shape[1]), jnp.bfloat16)
    return ((dot_nt(ones, high) + dot_nt(ones, low)) * (1.0 / block.shape[1]))[0:1]


def norm_chunks(blocks, norms, first):
    for c in (first, first + 1):
        for t in range(TILES):
            across = norms_across(blocks[TILES * c + t])
            for h in range(2):
                norms[c, pl.ds(2 * t + h, 1), :] = across[:, h * 128:(h + 1) * 128]


def block_of(r, i):
    return jnp.clip(r.sup[0, i] - r.first_block, 0, r.tgt.shape[0] - 1)


def start_columns(r, o, count):
    for a in range(count):
        block = r.tgt[count * o + a]
        down = jnp.sum(squares(block), axis=1, keepdims=True) * (-SCALE / block.shape[1])
        r.gcol[count * o + a] = jnp.broadcast_to(down, (BS, 128))


def row_group(r, it, g, chunks, place):
    for k in range(chunks):
        c = chunks * g + k
        for t in range(TILES):
            i = TILES * c + t
            block = block_of(r, i)
            dead = jnp.where(r.cnt[0, i] > 0, 0.0, floor_value)
            if it == 0:
                made = dot_nt(r.tgt[block], r.src[i]) * (2.0 * SCALE / r.src.shape[2])
                r.dots_qp[i] = made
            else:
                held = r.gall.at[it - 1, block // (4 * r.half), lax.rem(block // 4, r.half)]
                down = [lane_column(held[pl.ds(2 * lax.rem(block, 4) + h, 1), :]) for h in range(2)]
            for h in range(2):
                lanes = slice(h * 128, (h + 1) * 128)
                if it == 0:
                    products = lambda k: made[k:k + PART, lanes]
                    offsets = lambda k: r.gcol[block, k:k + PART, :]
                else:
                    products = lambda k: r.dots_qp[i, k:k + PART, lanes]
                    offsets = lambda k: down[k // 128][k % 128:k % 128 + PART]
                peak, total = tile_pairs(products, offsets)
                here = pl.ds(64 * k + 8 * (2 * t + h), 8)
                r.peaks[here, :] = peak + dead
                r.sums[here, :] = total
        at = pl.ds(64 * k, 64)
        place(c, log_sum(sublane_pairs(r.peaks.at[at], r.sums.at[at], 8, 8)))


def make_group(r, g, chunks):
    sublane = lax.broadcasted_iota(jnp.int32, (8, 128), 0)
    for k in range(chunks):
        c = chunks * g + k
        names = jnp.full((8, 128), -1, jnp.int32)
        for t in range(TILES):
            i = TILES * c + t
            block = block_of(r, i)
            r.dots_pq[i] = dot_nt(r.src[i], r.tgt[block]) * (2.0 * SCALE / r.src.shape[2])
            name = jnp.where(r.cnt[0, i] > 0, block, -1)
            names = jnp.where(lax.rem(sublane, TILES) == t, name, names)
        r.key[c] = names


def col_group(r, g, chunks):
    for k in range(chunks):
        c = chunks * g + k
        for t in range(TILES):
            i = TILES * c + t
            down = [lane_column(r.fall[c, pl.ds(2 * t + h, 1), :]) for h in range(2)]
            for h in range(2):
                peak, total = tile_pairs(
                    lambda k: r.dots_pq[i, k:k + PART, h * 128:(h + 1) * 128],
                    lambda k: down[k // 128][k % 128:k % 128 + PART])
                here = pl.ds(64 * k + 8 * (TILES * h + t), 8)
                r.peaks[here, :] = peak
                r.sums[here, :] = total
        at = pl.ds(64 * k, 64)
        r.lpart[c] = log_sum(sublane_pairs(r.peaks.at[at], r.sums.at[at], 8, 8))


def merge_columns(r, chunk, slot):
    for u in range(4):
        mine = jnp.where(r.key[...] == 4 * chunk + u, r.lpart[...], floor_value)
        peak = jnp.max(mine, axis=0)
        here = pl.ds(32 * slot + 8 * u, 8)
        r.peaks[here, :] = peak
        r.sums[here, :] = jnp.sum(jnp.exp2(mine - peak[None]), axis=0)
    at = pl.ds(32 * slot, 32)
    return log_sum(sublane_pairs(r.peaks.at[at], r.sums.at[at], 8, 4))


REFS = (
    "sup_hbm", "cnt_hbm", "src_hbm", "tgt_hbm", "ls_hbm", "lt_hbm", "f_out", "g_out", "sup", "cnt", "ls",
    "lt", "src", "tgt", "dots_qp", "dots_pq", "gcol", "peaks", "sums", "key", "fall", "lpart", "rnorm",
    "cnorm", "first", "second", "stage", "pair", "ring", "gall", "tgt_sem", "src_sem", "slot_sem",
    "weight_sem", "first_send", "first_recv", "second_send", "second_recv", "pair_send", "pair_recv",
    "ring_send", "ring_recv", "back_send", "back_recv",
)


class Refs:
    pass


def kernel(n_row, n_col, *refs):
    r = Refs()
    for name, ref in zip(REFS, refs, strict=True):
        setattr(r, name, ref)
    side = math.isqrt(n_col)
    depth = n_row // 2
    my_row, my_col = lax.axis_index("row"), lax.axis_index("col")
    my_x, my_y = my_col // side, lax.rem(my_col, side)
    my_z, my_core = my_row // 2, lax.rem(my_row, 2)
    other = 1 - my_core
    r.first_block = my_col * r.tgt.shape[0]
    chunks = n_col // GROUPS
    r.half = half = r.gall.shape[2]

    tgt_part = r.tgt.shape[0] // TGT_PARTS

    def tgt_copy(o):
        here = pl.ds(o * tgt_part, tgt_part)
        return pltpu.make_async_copy(r.tgt_hbm.at[here], r.tgt.at[here], r.tgt_sem.at[o])

    for o in range(TGT_PARTS):
        tgt_copy(o).start()

    slot_copies = [
        pltpu.make_async_copy(r.sup_hbm, r.sup, r.slot_sem.at[0]),
        pltpu.make_async_copy(r.cnt_hbm, r.cnt, r.slot_sem.at[1])]
    for copy in slot_copies:
        copy.start()

    def src_copy(g):
        here = pl.ds(g * chunks * TILES, chunks * TILES)
        return pltpu.make_async_copy(r.src_hbm.at[here], r.src.at[here], r.src_sem.at[g])

    for g in range(GROUPS):
        src_copy(g).start()

    weight_copies = [
        pltpu.make_async_copy(r.ls_hbm, r.ls, r.weight_sem.at[0]),
        pltpu.make_async_copy(r.lt_hbm, r.lt, r.weight_sem.at[1])]
    for copy in weight_copies:
        copy.start()

    def on_x(o):
        return (my_row, lax.rem(my_x + o, side) * side + my_y)

    def on_y(o):
        return (my_row, my_x * side + lax.rem(my_y + o, side))

    def on_z(o):
        return (lax.rem(my_z + o, depth) * 2 + my_core, my_col)

    sibling = (my_z * 2 + other, my_col)
    barrier = pltpu.get_barrier_semaphore()
    for o in range(1, depth):
        pl.semaphore_signal(barrier, inc=1, device_id=on_z(o), device_id_type=MESH)
    for o in range(1, side):
        pl.semaphore_signal(barrier, inc=1, device_id=on_x(o), device_id_type=MESH)
        pl.semaphore_signal(barrier, inc=1, device_id=on_y(o), device_id_type=MESH)
    pl.semaphore_signal(barrier, inc=1, device_id=sibling, device_id_type=MESH)

    def place_of(g, which):
        x_now = lax.rem(g + which, 2) == 0
        return x_now, jnp.where(x_now, my_x, my_y)

    def row_copy(it, g, which, o):
        buffer, send, recv = (r.first, r.first_send, r.first_recv) if which == 0 else (
            r.second, r.second_send, r.second_recv)
        x_now, me = place_of(g, which)
        (row, x_col), (_, y_col) = on_x(o), on_y(o)
        here = buffer.at[it, me, pl.ds(g * chunks, chunks)]
        return pltpu.make_async_remote_copy(
            src_ref=here, dst_ref=here, send_sem=send.at[it, g, o], recv_sem=recv.at[it, g, me],
            device_id=(row, jnp.where(x_now, x_col, y_col)), device_id_type=MESH)

    def row_arrived(it, g, which):
        buffer, recv = (r.first, r.first_recv) if which == 0 else (r.second, r.second_recv)
        _, me = place_of(g, which)
        for o in range(1, side):
            slot = lax.rem(me + o, side)
            here = buffer.at[it, slot, pl.ds(g * chunks, chunks)]
            pltpu.make_async_copy(here, here, recv.at[it, g, slot]).wait()

    def row_merged(it, g, which):
        buffer = r.first if which == 0 else r.second
        return merged_logs([buffer[it, d, pl.ds(g * chunks, chunks)] for d in range(side)])

    def pair_copy(it):
        return pltpu.make_async_remote_copy(
            src_ref=r.stage.at[it], dst_ref=r.pair.at[it, my_core],
            send_sem=r.pair_send.at[it], recv_sem=r.pair_recv.at[it],
            device_id=sibling, device_id_type=MESH)

    def ring_copy(it, o):
        here = r.ring.at[it, my_z]
        return pltpu.make_async_remote_copy(
            src_ref=here, dst_ref=here, send_sem=r.ring_send.at[it, o], recv_sem=r.ring_recv.at[it, my_z],
            device_id=on_z(o), device_id_type=MESH)

    def back_copy(it):
        here = r.gall.at[it, my_core]
        return pltpu.make_async_remote_copy(
            src_ref=here, dst_ref=here, send_sem=r.back_send.at[it], recv_sem=r.back_recv.at[it],
            device_id=sibling, device_id_type=MESH)

    @pl.loop(0, TGT_PARTS)
    def _(o):
        tgt_copy(o).wait()
        start_columns(r, o, tgt_part)

    for copy in slot_copies:
        copy.wait()

    for it in range(ITERS):
        @pl.loop(0, GROUPS)
        def _(g):
            if it == 0:
                src_copy(g).wait()
            _, me = place_of(g, 0)

            def place(c, value):
                r.first[it, me, c] = value

            row_group(r, it, g, chunks, place)
            if it == 0:
                @pl.when(g == 0)
                def _():
                    pl.semaphore_wait(barrier, 2 * (side - 1) + depth)

            for o in range(1, side):
                row_copy(it, g, 0, o).start()

        @pl.loop(0, GROUPS)
        def _(g):
            if it == 0:
                @pl.when(g == 0)
                def _():
                    for copy in weight_copies:
                        copy.wait()

            row_arrived(it, g, 0)
            _, me = place_of(g, 1)
            r.second[it, me, pl.ds(g * chunks, chunks)] = row_merged(it, g, 0)
            for o in range(1, side):
                row_copy(it, g, 1, o).start()
            if it == 0:
                make_group(r, g, chunks)

        @pl.loop(0, GROUPS)
        def _(g):
            row_arrived(it, g, 1)
            here = pl.ds(g * chunks, chunks)
            r.fall[here] = r.ls[here] * LOG2E - row_merged(it, g, 1)
            col_group(r, g, chunks)

        for j in range(half):
            r.stage[it, j] = merge_columns(r, other * half + j, j)

        pair_copy(it).start()

        for j in range(half):
            r.pair[it, my_core, j] = merge_columns(r, my_core * half + j, j)

        pair_copy(it).wait_recv()
        r.ring[it, my_z] = merged_logs([r.pair[it, 0], r.pair[it, 1]])
        far_first = sorted(range(1, depth), key=lambda o: -min(o, depth - o))
        for o in far_first:
            ring_copy(it, o).start()

        if it == 0:
            pl.loop(0, half)(lambda c: norm_chunks(r.tgt, r.cnorm, 2 * c))

        if it == ITERS - 1:
            pl.loop(0, n_col // 2)(lambda c: norm_chunks(r.src, r.rnorm, 2 * c))
            r.f_out[...] = r.fall[...] * (1.0 / SCALE) + r.rnorm[...]

        @pl.loop(0, GROUPS)
        def _(g):
            for o in range(1, side):
                row_copy(it, g, 0, o).wait_send()
                row_copy(it, g, 1, o).wait_send()

        pair_copy(it).wait_send()

        for o in far_first:
            slot = lax.rem(my_z + o, depth)
            here = r.ring.at[it, slot]
            pltpu.make_async_copy(here, here, r.ring_recv.at[it, slot]).wait()
        r.gall[it, my_core] = (
            r.lt[pl.ds(my_core * half, half)] * LOG2E - merged_logs([r.ring[it, d] for d in range(depth)]))
        back_copy(it).start()

        def finish(core):
            if it == ITERS - 1:
                here = pl.ds(core * half, half)
                r.g_out[here] = r.gall[it, core] * (1.0 / SCALE) + r.cnorm[here]

        finish(my_core)
        for o in far_first:
            ring_copy(it, o).wait_send()
        back_copy(it).wait()
        finish(other)


def handed_on(f_from, g_from, f_to, g_to):
    f_to[...] = f_from[...]
    g_to[...] = g_from[...]


def on_device(n_row, n_col, source, target, log_source, log_target, support, counts):
    row_count = support.shape[0]
    embed = source.shape[1]
    col_count = target.shape[0] // BS
    side = math.isqrt(n_col)
    depth = n_row // 2
    f32 = jnp.float32
    vmem = pl.BlockSpec(memory_space=pltpu.VMEM)
    hbm = pl.BlockSpec(memory_space=pl.ANY)
    dma = pltpu.SemaphoreType.DMA
    row_shape, col_shape = (row_count // TILES, 8, 128), (col_count // TILES, 8, 128)
    half_shape = (col_count // TILES // 2, 8, 128)
    gathered = TILES * 16 * row_count // (TILES * GROUPS)
    f, g = pl.pallas_call(
        functools.partial(kernel, n_row, n_col),
        out_shape=(jax.ShapeDtypeStruct(row_shape, f32), jax.ShapeDtypeStruct(col_shape, f32)),
        in_specs=[hbm] * 6,
        out_specs=(vmem, vmem),
        scratch_shapes=[
            pltpu.SMEM((1, row_count), jnp.int32),
            pltpu.SMEM((1, row_count), jnp.int32),
            pltpu.VMEM(row_shape, f32),
            pltpu.VMEM(col_shape, f32),
            pltpu.VMEM((row_count, BS, embed), jnp.bfloat16),
            pltpu.VMEM((col_count, BS, embed), jnp.bfloat16),
            pltpu.VMEM((row_count, BS, BS), f32),
            pltpu.VMEM((row_count, BS, BS), f32),
            pltpu.VMEM((col_count, BS, 128), f32),
            pltpu.VMEM((gathered, 128), f32),
            pltpu.VMEM((gathered, 128), f32),
            pltpu.VMEM(row_shape, jnp.int32),
            pltpu.VMEM(row_shape, f32),
            pltpu.VMEM(row_shape, f32),
            pltpu.VMEM(row_shape, f32),
            pltpu.VMEM(col_shape, f32),
            pltpu.VMEM((ITERS, side) + row_shape, f32),
            pltpu.VMEM((ITERS, side) + row_shape, f32),
            pltpu.VMEM((ITERS,) + half_shape, f32),
            pltpu.VMEM((ITERS, 2) + half_shape, f32),
            pltpu.VMEM((ITERS, depth) + half_shape, f32),
            pltpu.VMEM((ITERS, 2) + half_shape, f32),
            dma((TGT_PARTS,)),
            dma((GROUPS,)),
            dma((2,)),
            dma((2,)),
            dma((ITERS, GROUPS, side)), dma((ITERS, GROUPS, side)),
            dma((ITERS, GROUPS, side)), dma((ITERS, GROUPS, side)),
            dma((ITERS,)), dma((ITERS,)),
            dma((ITERS, depth)), dma((ITERS, depth)),
            dma((ITERS,)), dma((ITERS,)),
        ],
        compiler_params=pltpu.CompilerParams(
            collective_id=0, has_side_effects=True, vmem_limit_bytes=56 * 1024 * 1024),
    )(
        support.T, counts.T,
        source.reshape(row_count, BS, embed), target.reshape(col_count, BS, embed),
        log_source.reshape(row_shape), log_target.reshape(col_shape),
    )
    f, g = pl.pallas_call(
        handed_on,
        out_shape=(jax.ShapeDtypeStruct(row_shape, f32), jax.ShapeDtypeStruct(col_shape, f32)),
        in_specs=[vmem, vmem],
        out_specs=(vmem, vmem),
    )(f, g)
    return f.reshape(-1), g.reshape(-1)


def solution(mesh):
    placed = (P("row", None), P("col", None), P("row"), P("col"), P("row", "col"), P("row", "col"))
    body = functools.partial(on_device, mesh.shape["row"], mesh.shape["col"])
    return jax.shard_map(
        body, mesh=mesh, in_specs=placed, out_specs=(P("row"), P("col")), check_vma=False
    )
```

```python
import functools
import math

import jax
import jax.numpy as jnp
from jax import lax
from jax.experimental import pallas as pl
from jax.experimental.pallas import tpu as pltpu
from jax.sharding import PartitionSpec as P

BS = 256
ITERS = 2
entropic = 0.1
floor_value = -1e30
LOG2E = math.log2(math.e)
SCALE = LOG2E / entropic
MESH = pl.DeviceIdType.MESH
TILES = 4
GROUPS = 4
TGT_PARTS = 2
PART = 64


def dot_nt(a, b):
    return lax.dot_general(a, b, (((1,), (1,)), ((), ())), preferred_element_type=jnp.float32)


def lane_column(row):
    return jnp.transpose(jnp.broadcast_to(row, (128, 128)))


def tree(op, parts):
    parts = list(parts)
    while len(parts) > 1:
        paired = [op(a, b) for a, b in zip(parts[::2], parts[1::2])]
        parts = paired + parts[len(parts) - len(parts) % 2:]
    return parts[0]


def merged(pairs):
    peak = tree(jnp.maximum, [p for p, _ in pairs])
    return peak, tree(jnp.add, [s * jnp.exp2(p - peak) for p, s in pairs])


def log_sum(pair):
    return pair[0] + LOG2E * jnp.log(pair[1])


def merged_logs(parts):
    peak = tree(jnp.maximum, parts)
    return peak + LOG2E * jnp.log(tree(jnp.add, [jnp.exp2(part - peak) for part in parts]))


def tile_pairs(products, offsets):
    pairs = []
    for k in range(0, BS, PART):
        scores = (products(k) + offsets(k)).reshape(PART // 8, 8, 128)
        peak = jnp.max(scores, axis=0)
        pairs.append((peak, jnp.sum(jnp.exp2(scores - peak[None]), axis=0)))
    return merged(pairs)


def sublane_pairs(peaks, sums, count, stride):
    return merged([
        (peaks[pl.ds(s, count, stride=stride), :], sums[pl.ds(s, count, stride=stride), :])
        for s in range(stride)])


def squares(block):
    wide = block.astype(jnp.float32)
    return wide * wide


def norms_across(block):
    square = squares(block)
    high = square.astype(jnp.bfloat16)
    low = (square - high.astype(jnp.float32)).astype(jnp.bfloat16)
    ones = jnp.ones((8, block.shape[1]), jnp.bfloat16)
    return ((dot_nt(ones, high) + dot_nt(ones, low)) * (1.0 / block.shape[1]))[0:1]


def norm_chunks(blocks, norms, first):
    for c in (first, first + 1):
        for t in range(TILES):
            across = norms_across(blocks[TILES * c + t])
            for h in range(2):
                norms[c, pl.ds(2 * t + h, 1), :] = across[:, h * 128:(h + 1) * 128]


def block_of(r, i):
    return jnp.clip(r.sup[0, i] - r.first_block, 0, r.tgt.shape[0] - 1)


def start_columns(r, o, count):
    for a in range(count):
        block = r.tgt[count * o + a]
        square = squares(block)
        if a % 2 == 0:
            down = jnp.broadcast_to(jnp.sum(square, axis=1, keepdims=True), (BS, 128))
        else:
            high = square.astype(jnp.bfloat16)
            low = (square - high.astype(jnp.float32)).astype(jnp.bfloat16)
            ones = jnp.ones((block.shape[1], 128), jnp.bfloat16)
            down = (jnp.dot(high, ones, preferred_element_type=jnp.float32)
                    + jnp.dot(low, ones, preferred_element_type=jnp.float32))
        r.gcol[count * o + a] = down * (-SCALE / block.shape[1])


def row_group(r, it, g, chunks, place):
    for k in range(chunks):
        c = chunks * g + k
        for t in range(TILES):
            i = TILES * c + t
            block = block_of(r, i)
            dead = jnp.where(r.cnt[0, i] > 0, 0.0, floor_value)
            if it == 0:
                made = dot_nt(r.tgt[block], r.src[i]) * (2.0 * SCALE / r.src.shape[2])
                r.dots_qp[i] = made
            else:
                held = r.gall.at[it - 1, block // (4 * r.half), lax.rem(block // 4, r.half)]
                down = [lane_column(held[pl.ds(2 * lax.rem(block, 4) + h, 1), :]) for h in range(2)]
            for h in range(2):
                lanes = slice(h * 128, (h + 1) * 128)
                if it == 0:
                    products = lambda k: made[k:k + PART, lanes]
                    offsets = lambda k: r.gcol[block, k:k + PART, :]
                else:
                    products = lambda k: r.dots_qp[i, k:k + PART, lanes]
                    offsets = lambda k: down[k // 128][k % 128:k % 128 + PART]
                peak, total = tile_pairs(products, offsets)
                here = pl.ds(64 * k + 8 * (2 * t + h), 8)
                r.peaks[here, :] = peak + dead
                r.sums[here, :] = total
        at = pl.ds(64 * k, 64)
        place(c, log_sum(sublane_pairs(r.peaks.at[at], r.sums.at[at], 8, 8)))


def make_group(r, g, chunks):
    sublane = lax.broadcasted_iota(jnp.int32, (8, 128), 0)
    for k in range(chunks):
        c = chunks * g + k
        names = jnp.full((8, 128), -1, jnp.int32)
        for t in range(TILES):
            i = TILES * c + t
            block = block_of(r, i)
            r.dots_pq[i] = dot_nt(r.src[i], r.tgt[block]) * (2.0 * SCALE / r.src.shape[2])
            name = jnp.where(r.cnt[0, i] > 0, block, -1)
            names = jnp.where(lax.rem(sublane, TILES) == t, name, names)
        r.key[c] = names


def col_group(r, g, chunks):
    for k in range(chunks):
        c = chunks * g + k
        for t in range(TILES):
            i = TILES * c + t
            down = [lane_column(r.fall[c, pl.ds(2 * t + h, 1), :]) for h in range(2)]
            for h in range(2):
                peak, total = tile_pairs(
                    lambda k: r.dots_pq[i, k:k + PART, h * 128:(h + 1) * 128],
                    lambda k: down[k // 128][k % 128:k % 128 + PART])
                here = pl.ds(64 * k + 8 * (TILES * h + t), 8)
                r.peaks[here, :] = peak
                r.sums[here, :] = total
        at = pl.ds(64 * k, 64)
        r.lpart[c] = log_sum(sublane_pairs(r.peaks.at[at], r.sums.at[at], 8, 8))


def merge_columns(r, chunk, slot):
    for u in range(4):
        mine = jnp.where(r.key[...] == 4 * chunk + u, r.lpart[...], floor_value)
        peak = jnp.max(mine, axis=0)
        here = pl.ds(32 * slot + 8 * u, 8)
        r.peaks[here, :] = peak
        r.sums[here, :] = jnp.sum(jnp.exp2(mine - peak[None]), axis=0)
    at = pl.ds(32 * slot, 32)
    return log_sum(sublane_pairs(r.peaks.at[at], r.sums.at[at], 8, 4))


REFS = (
    "sup_hbm", "cnt_hbm", "src_hbm", "tgt_hbm", "ls_hbm", "lt_hbm", "f_out", "g_out", "sup", "cnt", "ls",
    "lt", "src", "tgt", "dots_qp", "dots_pq", "gcol", "peaks", "sums", "key", "fall", "lpart", "rnorm",
    "cnorm", "first", "second", "stage", "pair", "ring", "gall", "tgt_sem", "src_sem", "slot_sem",
    "weight_sem", "first_send", "first_recv", "second_send", "second_recv", "pair_send", "pair_recv",
    "ring_send", "ring_recv", "back_send", "back_recv",
)


class Refs:
    pass


def far_first(ring):
    return sorted(range(1, ring), key=lambda o: -min(o, ring - o))


def kernel(n_row, n_col, *refs):
    r = Refs()
    for name, ref in zip(REFS, refs, strict=True):
        setattr(r, name, ref)
    side = math.isqrt(n_col)
    depth = n_row // 2
    my_row, my_col = lax.axis_index("row"), lax.axis_index("col")
    my_x, my_y = my_col // side, lax.rem(my_col, side)
    my_z, my_core = my_row // 2, lax.rem(my_row, 2)
    other = 1 - my_core
    r.first_block = my_col * r.tgt.shape[0]
    chunks = n_col // GROUPS
    r.half = half = r.gall.shape[2]

    tgt_part = r.tgt.shape[0] // TGT_PARTS

    def tgt_copy(o):
        here = pl.ds(o * tgt_part, tgt_part)
        return pltpu.make_async_copy(r.tgt_hbm.at[here], r.tgt.at[here], r.tgt_sem.at[o])

    for o in range(TGT_PARTS):
        tgt_copy(o).start()

    slot_copies = [
        pltpu.make_async_copy(r.sup_hbm, r.sup, r.slot_sem.at[0]),
        pltpu.make_async_copy(r.cnt_hbm, r.cnt, r.slot_sem.at[1])]
    for copy in slot_copies:
        copy.start()

    def src_copy(g):
        here = pl.ds(g * chunks * TILES, chunks * TILES)
        return pltpu.make_async_copy(r.src_hbm.at[here], r.src.at[here], r.src_sem.at[g])

    for g in range(GROUPS):
        src_copy(g).start()

    weight_copies = [
        pltpu.make_async_copy(r.ls_hbm, r.ls, r.weight_sem.at[0]),
        pltpu.make_async_copy(r.lt_hbm, r.lt, r.weight_sem.at[1])]
    for copy in weight_copies:
        copy.start()

    def on_x(o):
        return (my_row, lax.rem(my_x + o, side) * side + my_y)

    def on_y(o):
        return (my_row, my_x * side + lax.rem(my_y + o, side))

    def on_z(o):
        return (lax.rem(my_z + o, depth) * 2 + my_core, my_col)

    sibling = (my_z * 2 + other, my_col)
    barrier = pltpu.get_barrier_semaphore()
    for o in range(1, depth):
        pl.semaphore_signal(barrier, inc=1, device_id=on_z(o), device_id_type=MESH)
    for o in range(1, side):
        pl.semaphore_signal(barrier, inc=1, device_id=on_x(o), device_id_type=MESH)
        pl.semaphore_signal(barrier, inc=1, device_id=on_y(o), device_id_type=MESH)
    pl.semaphore_signal(barrier, inc=1, device_id=sibling, device_id_type=MESH)

    def place_of(g, which):
        x_now = lax.rem(g + which, 2) == 0
        return x_now, jnp.where(x_now, my_x, my_y)

    def row_copy(it, g, which, o):
        buffer, send, recv = (r.first, r.first_send, r.first_recv) if which == 0 else (
            r.second, r.second_send, r.second_recv)
        x_now, me = place_of(g, which)
        (row, x_col), (_, y_col) = on_x(o), on_y(o)
        here = buffer.at[it, me, pl.ds(g * chunks, chunks)]
        return pltpu.make_async_remote_copy(
            src_ref=here, dst_ref=here, send_sem=send.at[it, g, o], recv_sem=recv.at[it, g, me],
            device_id=(row, jnp.where(x_now, x_col, y_col)), device_id_type=MESH)

    def row_arrived(it, g, which):
        buffer, recv = (r.first, r.first_recv) if which == 0 else (r.second, r.second_recv)
        _, me = place_of(g, which)
        for o in range(1, side):
            slot = lax.rem(me + o, side)
            here = buffer.at[it, slot, pl.ds(g * chunks, chunks)]
            pltpu.make_async_copy(here, here, recv.at[it, g, slot]).wait()

    def row_merged(it, g, which):
        buffer = r.first if which == 0 else r.second
        return merged_logs([buffer[it, d, pl.ds(g * chunks, chunks)] for d in range(side)])

    def pair_copy(it):
        return pltpu.make_async_remote_copy(
            src_ref=r.stage.at[it], dst_ref=r.pair.at[it, my_core],
            send_sem=r.pair_send.at[it], recv_sem=r.pair_recv.at[it],
            device_id=sibling, device_id_type=MESH)

    def ring_copy(it, o):
        here = r.ring.at[it, my_z]
        return pltpu.make_async_remote_copy(
            src_ref=here, dst_ref=here, send_sem=r.ring_send.at[it, o], recv_sem=r.ring_recv.at[it, my_z],
            device_id=on_z(o), device_id_type=MESH)

    def back_copy(it):
        here = r.gall.at[it, my_core]
        return pltpu.make_async_remote_copy(
            src_ref=here, dst_ref=here, send_sem=r.back_send.at[it], recv_sem=r.back_recv.at[it],
            device_id=sibling, device_id_type=MESH)

    @pl.loop(0, TGT_PARTS)
    def _(o):
        tgt_copy(o).wait()
        start_columns(r, o, tgt_part)

    for copy in slot_copies:
        copy.wait()

    for it in range(ITERS):
        @pl.loop(0, GROUPS)
        def _(g):
            if it == 0:
                src_copy(g).wait()
            _, me = place_of(g, 0)

            def place(c, value):
                r.first[it, me, c] = value

            row_group(r, it, g, chunks, place)
            if it == 0:
                @pl.when(g == 0)
                def _():
                    pl.semaphore_wait(barrier, 2 * (side - 1) + depth)

            for o in far_first(side):
                row_copy(it, g, 0, o).start()

        @pl.loop(0, GROUPS)
        def _(g):
            if it == 0:
                @pl.when(g == 0)
                def _():
                    for copy in weight_copies:
                        copy.wait()

            row_arrived(it, g, 0)
            _, me = place_of(g, 1)
            r.second[it, me, pl.ds(g * chunks, chunks)] = row_merged(it, g, 0)
            for o in far_first(side):
                row_copy(it, g, 1, o).start()
            if it == 0:
                make_group(r, g, chunks)

        @pl.loop(0, GROUPS)
        def _(g):
            row_arrived(it, g, 1)
            here = pl.ds(g * chunks, chunks)
            r.fall[here] = r.ls[here] * LOG2E - row_merged(it, g, 1)
            col_group(r, g, chunks)

        for j in range(half):
            r.stage[it, j] = merge_columns(r, other * half + j, j)

        pair_copy(it).start()

        for j in range(half):
            r.pair[it, my_core, j] = merge_columns(r, my_core * half + j, j)

        pair_copy(it).wait_recv()
        r.ring[it, my_z] = merged_logs([r.pair[it, 0], r.pair[it, 1]])
        for o in far_first(depth):
            ring_copy(it, o).start()

        if it == 0:
            pl.loop(0, half)(lambda c: norm_chunks(r.tgt, r.cnorm, 2 * c))

        if it == ITERS - 1:
            pl.loop(0, n_col // 2)(lambda c: norm_chunks(r.src, r.rnorm, 2 * c))
            r.f_out[...] = r.fall[...] * (1.0 / SCALE) + r.rnorm[...]

        @pl.loop(0, GROUPS)
        def _(g):
            for o in range(1, side):
                row_copy(it, g, 0, o).wait_send()
                row_copy(it, g, 1, o).wait_send()

        pair_copy(it).wait_send()

        for o in far_first(depth):
            slot = lax.rem(my_z + o, depth)
            here = r.ring.at[it, slot]
            pltpu.make_async_copy(here, here, r.ring_recv.at[it, slot]).wait()
        r.gall[it, my_core] = (
            r.lt[pl.ds(my_core * half, half)] * LOG2E - merged_logs([r.ring[it, d] for d in range(depth)]))
        back_copy(it).start()

        def finish(core):
            if it == ITERS - 1:
                here = pl.ds(core * half, half)
                r.g_out[here] = r.gall[it, core] * (1.0 / SCALE) + r.cnorm[here]

        finish(my_core)
        for o in far_first(depth):
            ring_copy(it, o).wait_send()
        back_copy(it).wait()
        finish(other)


def handed_on(f_from, g_from, f_to, g_to):
    f_to[...] = f_from[...]
    g_to[...] = g_from[...]


def on_device(n_row, n_col, source, target, log_source, log_target, support, counts):
    row_count = support.shape[0]
    embed = source.shape[1]
    col_count = target.shape[0] // BS
    side = math.isqrt(n_col)
    depth = n_row // 2
    f32 = jnp.float32
    vmem = pl.BlockSpec(memory_space=pltpu.VMEM)
    hbm = pl.BlockSpec(memory_space=pl.ANY)
    dma = pltpu.SemaphoreType.DMA
    row_shape, col_shape = (row_count // TILES, 8, 128), (col_count // TILES, 8, 128)
    half_shape = (col_count // TILES // 2, 8, 128)
    gathered = TILES * 16 * row_count // (TILES * GROUPS)
    f, g = pl.pallas_call(
        functools.partial(kernel, n_row, n_col),
        out_shape=(jax.ShapeDtypeStruct(row_shape, f32), jax.ShapeDtypeStruct(col_shape, f32)),
        in_specs=[hbm] * 6,
        out_specs=(vmem, vmem),
        scratch_shapes=[
            pltpu.SMEM((1, row_count), jnp.int32),
            pltpu.SMEM((1, row_count), jnp.int32),
            pltpu.VMEM(row_shape, f32),
            pltpu.VMEM(col_shape, f32),
            pltpu.VMEM((row_count, BS, embed), jnp.bfloat16),
            pltpu.VMEM((col_count, BS, embed), jnp.bfloat16),
            pltpu.VMEM((row_count, BS, BS), f32),
            pltpu.VMEM((row_count, BS, BS), f32),
            pltpu.VMEM((col_count, BS, 128), f32),
            pltpu.VMEM((gathered, 128), f32),
            pltpu.VMEM((gathered, 128), f32),
            pltpu.VMEM(row_shape, jnp.int32),
            pltpu.VMEM(row_shape, f32),
            pltpu.VMEM(row_shape, f32),
            pltpu.VMEM(row_shape, f32),
            pltpu.VMEM(col_shape, f32),
            pltpu.VMEM((ITERS, side) + row_shape, f32),
            pltpu.VMEM((ITERS, side) + row_shape, f32),
            pltpu.VMEM((ITERS,) + half_shape, f32),
            pltpu.VMEM((ITERS, 2) + half_shape, f32),
            pltpu.VMEM((ITERS, depth) + half_shape, f32),
            pltpu.VMEM((ITERS, 2) + half_shape, f32),
            dma((TGT_PARTS,)),
            dma((GROUPS,)),
            dma((2,)),
            dma((2,)),
            dma((ITERS, GROUPS, side)), dma((ITERS, GROUPS, side)),
            dma((ITERS, GROUPS, side)), dma((ITERS, GROUPS, side)),
            dma((ITERS,)), dma((ITERS,)),
            dma((ITERS, depth)), dma((ITERS, depth)),
            dma((ITERS,)), dma((ITERS,)),
        ],
        compiler_params=pltpu.CompilerParams(
            collective_id=0, has_side_effects=True, vmem_limit_bytes=56 * 1024 * 1024),
    )(
        support.T, counts.T,
        source.reshape(row_count, BS, embed), target.reshape(col_count, BS, embed),
        log_source.reshape(row_shape), log_target.reshape(col_shape),
    )
    f, g = pl.pallas_call(
        handed_on,
        out_shape=(jax.ShapeDtypeStruct(row_shape, f32), jax.ShapeDtypeStruct(col_shape, f32)),
        in_specs=[vmem, vmem],
        out_specs=(vmem, vmem),
    )(f, g)
    return f.reshape(-1), g.reshape(-1)


def solution(mesh):
    placed = (P("row", None), P("col", None), P("row"), P("col"), P("row", "col"), P("row", "col"))
    body = functools.partial(on_device, mesh.shape["row"], mesh.shape["col"])
    return jax.shard_map(
        body, mesh=mesh, in_specs=placed, out_specs=(P("row"), P("col")), check_vma=False
    )
```
